32 devices in a mesh: row: 4 (over x, core), col: 8 (over z, y).
Axes of the slice: x: 2, y: 2, z: 4, core: 2. Of those that a mesh axis runs over, the one named last changes fastest.
Arguments:
- block_in: bfloat16 [4096, 2048], P('col', 'row'), may hold values from -6 to 6
- cotangent: bfloat16 [4096, 2048], P('col', 'row'), may hold values from -6 to 6
- segments: int32 [4096], P('row'), may hold values from 0 to 31, never falling along the last dimension, each value on 1 to 1024 neighbouring positions
- w_query: bfloat16 [2048, 2048], P('row', 'col'), may hold values from -0.125 to 0.125
- w_key: bfloat16 [2048, 2048], P('row', 'col'), may hold values from -0.125 to 0.125
- w_value: bfloat16 [2048, 4096], P('row', 'col'), may hold values from -0.125 to 0.125
- w_gate: bfloat16 [2048, 4096], P('row', 'col'), may hold values from -0.125 to 0.125
- w_out: bfloat16 [4096, 2048], P('col', 'row'), may hold values from -0.09375 to 0.09375
- w_up: bfloat16 [2048, 4096], P('row', 'col'), may hold values from -0.125 to 0.125
- w_down: bfloat16 [4096, 2048], P('col', 'row'), may hold values from -0.09375 to 0.09375
- retention_norm_gain: float32 [2048], P('row'), may hold values from 0.25 to 1.75
- retention_norm_bias: float32 [2048], P('row'), may hold values from -3 to 3
- feedforward_norm_gain: float32 [2048], P('row'), may hold values from 0.25 to 1.75
- feedforward_norm_bias: float32 [2048], P('row'), may hold values from -3 to 3
Outputs:
- block_out: bfloat16 [4096, 2048], P('col', 'row')
- grad_in: float32 [4096, 2048], P('col', 'row')
- grad_query: float32 [2048, 2048], P('row', 'col')
- grad_key: float32 [2048, 2048], P('row', 'col')
- grad_value: float32 [2048, 4096], P('row', 'col')
- grad_gate: float32 [2048, 4096], P('row', 'col')
- grad_out: float32 [4096, 2048], P('col', 'row')
- grad_up: float32 [2048, 4096], P('row', 'col')
- grad_down: float32 [4096, 2048], P('col', 'row')
- grad_attn_gain: float32 [2048], P('row')
- grad_attn_bias: float32 [2048], P('row')
- grad_ffn_gain: float32 [2048], P('row')
- grad_ffn_bias: float32 [2048], P('row')
The draws below stay inside these ranges and needn't reach their ends.
Inputs may be any that keep to these rules, and one draw needn't show every extreme that they name: `segments`: segment numbers never fall along the tokens; a document holds 1 to 1024 tokens.
All inputs are finite; a program needn't handle non-finite values.
Results may differ from the reference program's by a relative error of at most 0.014.
The reference program's roundings to bfloat16 on the way count: a program that leaves them out, or rounds other values in their place, can miss the bound.
Values may be sent and summed in bfloat16 or wider, within the bound.
No kernel may reach another device: no remote copies, remote signals or barrier semaphores. Data moves between devices by JAX's collectives and lax.ppermute only.
A program may use at most 320 MiB of HBM per device.

```python
import math
import jax
import jax.numpy as jnp
import numpy as np
from jax import lax

D = 2048
HEADS = 8
HK = 256
HV = 512
FF = 4096
SEQ = 1024
SPAN = 512
KD = 2048
VD = 4096
TOKENS = 4096
DOCS = 32


def shard_levels(own_key, shape, cuts, least, largest):
    def one(axis_at, blocks):
        steps = jax.random.uniform(jax.random.fold_in(jax.random.fold_in(own_key, 6), axis_at), (blocks,), jnp.float32, least / len(cuts), largest / len(cuts))
        return jnp.repeat(jnp.exp(steps), shape[axis_at] // blocks).reshape((-1,) + (1,) * (len(shape) - axis_at - 1))

    gain = one(*cuts[0])
    for cut in cuts[1:]:
        gain = gain * one(*cut)
    return gain


def length_profile(number_of, total, bound, lean):
    portions = [(1 << 20) // math.isqrt(standing ** lean) + 1 for standing in range(2, number_of + 1)]
    rest, holding = total - bound - (number_of - 1), [1] * (number_of - 1)
    while rest > 0:
        movable = [i for i in range(number_of - 1) if holding[i] < bound]
        mass, budget = sum([portions[i] for i in movable]), rest
        for i in movable:
            more = min(bound - holding[i], max(1, budget * portions[i] // mass), rest)
            holding[i] = holding[i] + more
            rest = rest - more
    return np.array([bound] + holding)


def uneven(own_key, amount, total, limit, slope):
    if amount == 2:
        one = jax.random.randint(own_key, (), max(1, total - limit), min(limit, total - 1) + 1)
        return jnp.stack([one, total - one])
    sizes = jnp.asarray(length_profile(amount, total, limit, slope), jnp.int32)
    pairs = (amount - 1) // 2
    source_of, receiver = sizes[1:1 + 2 * pairs:2], sizes[2:2 + 2 * pairs:2]
    room = jnp.minimum(source_of - 1, limit - receiver)
    passed = jax.random.randint(jax.random.fold_in(own_key, 1), (pairs,), 0, 1 << 20) % (room + 1)
    sizes = sizes.at[1:1 + 2 * pairs:2].set(source_of - passed).at[2:2 + 2 * pairs:2].set(receiver + passed)
    return sizes[jax.random.permutation(jax.random.fold_in(own_key, 2), amount)]


def gaussian(own_key, extent, spread, limit, shards=(), held_as=jnp.bfloat16):
    loudness = shard_levels(own_key, extent, shards, -0.22, 0.18) if shards else 1.0
    array = jax.random.normal(own_key, extent, jnp.float32) * spread * loudness
    return jnp.minimum(jnp.maximum(array, -limit), limit).astype(held_as)


def setup_inputs(seed: int = 0) -> dict:
    key_list = jax.random.split(jax.random.key(seed), 15)
    return {
        "block_in": gaussian(key_list[0], (TOKENS, D), 1.0, 6.0, ((0, 8), (1, 4))),
        "cotangent": gaussian(key_list[1], (TOKENS, D), 1.0, 6.0, ((0, 8), (1, 4))),
        "segments": jnp.searchsorted(jnp.cumsum(uneven(key_list[2], DOCS, TOKENS, SEQ, 2)), jnp.arange(TOKENS), side="right").astype(jnp.int32),
        "w_query": gaussian(key_list[3], (D, KD), D ** -0.5, 0.125, ((0, 4), (1, 8))),
        "w_key": gaussian(key_list[4], (D, KD), D ** -0.5, 0.125, ((0, 4), (1, 8))),
        "w_value": gaussian(key_list[5], (D, VD), D ** -0.5, 0.125, ((0, 4), (1, 8))),
        "w_gate": gaussian(key_list[6], (D, VD), D ** -0.5, 0.125, ((0, 4), (1, 8))),
        "w_out": gaussian(key_list[7], (VD, D), VD ** -0.5, 0.09375, ((0, 8), (1, 4))),
        "w_up": gaussian(key_list[8], (D, FF), D ** -0.5, 0.125, ((0, 4), (1, 8))),
        "w_down": gaussian(key_list[9], (FF, D), FF ** -0.5, 0.09375, ((0, 8), (1, 4))),
        "retention_norm_gain": jnp.clip(1.0 + 0.15 * jax.random.normal(key_list[10], (D,), jnp.float32), 0.25, 1.75),
        "retention_norm_bias": gaussian(key_list[11], (D,), 0.5, 3.0, ((0, 4),), jnp.float32),
        "feedforward_norm_gain": jnp.clip(1.0 + 0.15 * jax.random.normal(key_list[12], (D,), jnp.float32), 0.25, 1.75),
        "feedforward_norm_bias": gaussian(key_list[13], (D,), 0.5, 3.0, ((0, 4),), jnp.float32),
    }


@jax.custom_vjp
def low(v):
    return lax.optimization_barrier(v.astype(jnp.bfloat16)).astype(jnp.float32)

@jax.custom_vjp
def low_back(v):
    return v

def low_keep(v):
    return (low(v), None)

def low_pass(kept, grad):
    return (grad,)

def back_keep(v):
    return (v, None)

def back_low(kept, grad):
    return (low(grad),)
low.defvjp(low_keep, low_pass)
low_back.defvjp(back_keep, back_low)
eps_norm = 1e-05
group_eps = 0.25
highest = lax.Precision.HIGHEST

def matmul(left, right):
    return jnp.dot(left, right, precision=highest)

def layer_norm(residual_stream, norm_gain, norm_offset):
    row_average = lax.optimization_barrier(jnp.mean(residual_stream, axis=-1, keepdims=True))
    var = lax.optimization_barrier(jnp.mean(jnp.square(residual_stream - row_average), axis=-1, keepdims=True))
    return (residual_stream - row_average) * lax.rsqrt(var + eps_norm) * norm_gain + norm_offset

def decay_block(first_branch, seg_query, seg_keys, loggam):
    rows = first_branch + lax.iota(jnp.int32, seg_query.shape[0])
    cols = lax.iota(jnp.int32, seg_keys.shape[0])
    gap = rows[:, None] - cols[None, :]
    inside = (gap >= 0) & (seg_query[:, None] == seg_keys[None, :])
    return jnp.where(inside, jnp.exp(jnp.maximum(gap, 0).astype(jnp.float32) * loggam), jnp.float32(0.0))

def retain_head(query, keys, values, seg, loggam):
    scale = HK ** (-0.5)

    def one_block(index):
        first_branch = index * SPAN
        q_blk = lax.dynamic_slice_in_dim(query, first_branch, SPAN, 0)
        seg_q = lax.dynamic_slice_in_dim(seg, first_branch, SPAN, 0)
        raw = low_back(jnp.dot(q_blk, keys.T, precision=highest))
        weights = low(raw * scale * decay_block(first_branch, seg_q, seg, loggam))
        return low_back(jnp.dot(weights, values, precision=highest))
    outs = lax.map(jax.checkpoint(one_block), jnp.arange(SEQ // SPAN, dtype=jnp.int32))
    retained = outs.reshape(SEQ, HV)
    row_average = lax.optimization_barrier(jnp.mean(retained, axis=-1, keepdims=True))
    var = lax.optimization_barrier(jnp.mean(jnp.square(retained - row_average), axis=-1, keepdims=True))
    return (retained - row_average) * lax.rsqrt(var + group_eps)

def layer(block, w_query, w_key, w_value, w_gate, w_out, w_up, w_down, retention_norm_gain, retention_norm_bias, feedforward_norm_gain, feedforward_norm_bias, seg_group):
    tokens = block.shape[0]
    groups = tokens // SEQ
    first_normed = low(layer_norm(block, retention_norm_gain, retention_norm_bias))
    query = low_back(low(matmul(first_normed, w_query))).reshape(groups, SEQ, HK, HEADS)
    keys = low_back(low(matmul(first_normed, w_key))).reshape(groups, SEQ, HK, HEADS)
    values = low_back(low(matmul(first_normed, w_value))).reshape(groups, SEQ, HV, HEADS)
    gate = low_back(matmul(first_normed, w_gate))
    head_ids = jnp.arange(HEADS, dtype=jnp.int32).astype(jnp.float32)
    loggam = jnp.log1p(-jnp.exp2(-5.0 - head_ids))
    over_heads = jax.vmap(retain_head, in_axes=(2, 2, 2, None, 0), out_axes=2)
    over_seqs = jax.vmap(over_heads, in_axes=(0, 0, 0, 0, None), out_axes=0)
    normed = low_back(low(over_seqs(query, keys, values, seg_group, loggam))).reshape(tokens, HEADS * HV)
    hidden = low(gate * jax.nn.sigmoid(gate) * normed)
    middle = block + low_back(matmul(hidden, w_out))
    second_normed = low(layer_norm(middle, feedforward_norm_gain, feedforward_norm_bias))
    pre = low_back(matmul(second_normed, w_up))
    act = low(jax.nn.gelu(pre, approximate=False))
    return middle + low_back(matmul(act, w_down))

def reference(block_in, cotangent, segments, w_query, w_key, w_value, w_gate, w_out, w_up, w_down, retention_norm_gain, retention_norm_bias, feedforward_norm_gain, feedforward_norm_bias):
    weights = (w_query.astype(jnp.float32), w_key.astype(jnp.float32), w_value.astype(jnp.float32), w_gate.astype(jnp.float32), w_out.astype(jnp.float32), w_up.astype(jnp.float32), w_down.astype(jnp.float32), retention_norm_gain.astype(jnp.float32), retention_norm_bias.astype(jnp.float32), feedforward_norm_gain.astype(jnp.float32), feedforward_norm_bias.astype(jnp.float32))
    group = 2 * SEQ
    count = block_in.shape[0] // group
    inputs = block_in.astype(jnp.float32).reshape(count, group, D)
    grads_top = cotangent.astype(jnp.float32).reshape(count, group, D)
    seg_all = segments.reshape(count, 2, SEQ)

    def step(carry, items):
        block, grad_top, seg_group = items

        def forward(part, *params):
            return layer(part, *params, seg_group)
        result, pull = jax.vjp(forward, block, *weights)
        pulled = pull(grad_top)
        carry = jax.tree.map(lambda total, extra: total + extra, carry, pulled[1:])
        return (carry, (result, pulled[0]))
    zeros = jax.tree.map(jnp.zeros_like, weights)
    totals, (results, grad_blocks) = lax.scan(step, zeros, (inputs, grads_top, seg_all))
    return (results.reshape(-1, D).astype(jnp.bfloat16), grad_blocks.reshape(-1, D), totals[0], totals[1], totals[2], totals[3], totals[4], totals[5], totals[6], totals[7], totals[8], totals[9], totals[10])
```

```python
import jax
import jax.numpy as jnp
from jax import lax
from jax.sharding import Mesh
from jax.sharding import PartitionSpec as P

HEADS = 8
EPS_NORM = 1e-05
EPS_GROUP = 0.25

ROW = ("x", "k")
GROUP = ("x", "k", "y")
EVERY = ("x", "k", "z", "y")
F32 = jnp.float32
BF16 = jnp.bfloat16


def dot(left, right, over):
    return lax.dot_general(left, right, (over, ((), ())), preferred_element_type=F32)


def swap(value, mask):
    return lax.ppermute(value, GROUP, [(i, i ^ mask) for i in range(8)])


def group_gather(part):
    near = jnp.stack([part, swap(part, 1), swap(part, 4), swap(part, 5)])
    near = near.reshape((2, 1, 2) + part.shape)
    return jnp.concatenate([near, swap(near, 2)], axis=1).reshape((-1,) + part.shape[1:])


def group_reduce(total):
    blocks = total.reshape(2, 2, 2, total.shape[0] // 8, total.shape[1])
    pair = (blocks[:, 0] + swap(blocks[:, 1].astype(BF16), 2).astype(F32)).astype(BF16)
    own = pair[0, 0].astype(F32)
    for i, j in ((0, 1), (1, 0), (1, 1)):
        own = own + swap(pair[i, j], 4 * i + j).astype(F32)
    return own


def row_exchange(parts):
    return lax.all_to_all(parts, ROW, split_axis=0, concat_axis=0, tiled=True)


def to_tokens(part):
    tokens, width = part.shape
    moved = row_exchange(part.reshape(4, tokens // 4, width))
    return moved.transpose(1, 0, 2).reshape(tokens // 4, 4 * width)


def from_tokens(part):
    tokens, width = part.shape
    moved = row_exchange(part.reshape(tokens, 4, width // 4).transpose(1, 0, 2))
    return moved.reshape(4 * tokens, width // 4)


def head_order(count):
    units = count // HEADS
    j = lax.iota(jnp.int32, count)
    target = (j % HEADS) * units + j // HEADS
    return (target[:, None] == lax.iota(jnp.int32, count)[None, :]).astype(BF16)


def layernorm(value, gain, bias):
    mean = jnp.mean(value, axis=1, keepdims=True)
    centered = value - mean
    inverse = lax.rsqrt(jnp.mean(centered * centered, axis=1, keepdims=True) + EPS_NORM)
    hat = centered * inverse
    return hat, inverse, (hat * gain + bias).astype(BF16)


def layernorm_back(grad, hat, inverse, gain):
    scaled = grad * gain
    first = jnp.mean(scaled, axis=1, keepdims=True)
    second = jnp.mean(scaled * hat, axis=1, keepdims=True)
    return (
        inverse * (scaled - first - hat * second),
        jnp.sum(grad * hat, axis=0),
        jnp.sum(grad, axis=0),
    )


def gelu_exact(value):
    return jax.nn.gelu(value, approximate=False)


def body(
    block_in,
    cotangent,
    segments,
    w_query,
    w_key,
    w_value,
    w_gate,
    w_out,
    w_up,
    w_down,
    retention_norm_gain,
    retention_norm_bias,
    feedforward_norm_gain,
    feedforward_norm_bias,
):
    depth = lax.axis_size("z")
    part = block_in.shape[1]
    width = 4 * part
    own = lax.axis_index(GROUP)
    plane = lax.axis_index("z")
    tokens = block_in.shape[0] // 4
    seq = 8 * tokens

    kq = w_query.shape[1] // HEADS
    kv = w_value.shape[1] // HEADS
    order_q = head_order(w_query.shape[1])
    order_v = head_order(w_value.shape[1])

    def by_head(weight, order):
        return dot(order, weight, ((0,), (1,))).astype(BF16).reshape(HEADS, -1, part)

    send_qkv = jnp.concatenate(
        [by_head(w_query, order_q), by_head(w_key, order_q), by_head(w_value, order_v)], axis=1
    )
    send_go = jnp.concatenate(
        [
            by_head(w_gate, order_v),
            dot(order_v, w_out, ((0,), (0,))).astype(BF16).reshape(HEADS, -1, part),
        ],
        axis=1,
    )

    def to_heads(send):
        got = lax.all_to_all(send, GROUP, split_axis=0, concat_axis=0, tiled=True)
        got = got.reshape(4, 2, send.shape[1], part).transpose(1, 2, 0, 3)
        return got.reshape(2, send.shape[1], width)

    got_qkv = to_heads(send_qkv)
    got_go = to_heads(send_go)
    mine_qkv = jnp.concatenate(
        [
            got_qkv[:, :kq].reshape(2 * kq, width),
            got_qkv[:, kq : 2 * kq].reshape(2 * kq, width),
            got_qkv[:, 2 * kq :].reshape(2 * kv, width),
        ],
        axis=0,
    )
    mine_go = jnp.concatenate(
        [got_go[:, :kv].reshape(2 * kv, width), got_go[:, kv:].reshape(2 * kv, width)], axis=0
    )

    def to_units(weight):
        got = row_exchange(weight.reshape(4, -1, part))
        return got.transpose(1, 0, 2).reshape(-1, width)

    mine_up = to_units(w_up.T)
    mine_down = to_units(w_down)

    def planes(mine):
        return lax.all_gather(mine, "z", axis=0, tiled=True)

    all_qkv = planes(mine_qkv)
    all_go = planes(mine_go).reshape(depth, 4 * kv, width)
    wt_gate = all_go[:, : 2 * kv].reshape(-1, width)
    wt_out = all_go[:, 2 * kv :].reshape(-1, width)
    wt_up = planes(mine_up)
    wt_down = planes(mine_down)

    params = lax.all_gather(
        jnp.stack(
            [
                retention_norm_gain,
                retention_norm_bias,
                feedforward_norm_gain,
                feedforward_norm_bias,
            ]
        ),
        ROW,
        axis=1,
        tiled=True,
    )
    stream = to_tokens(block_in).astype(F32)
    cot_own = to_tokens(cotangent)
    hat_one, inv_one, norm_one = layernorm(stream, params[0], params[1])
    x_one = group_gather(norm_one)
    cot = group_gather(cot_own)

    segs = lax.all_gather(segments, ROW, axis=0, tiled=True).reshape(depth, 8, tokens)
    ids = lax.iota(jnp.int32, 8) ^ own
    ids = (ids % 2) * 4 + ids // 2
    picked = (ids[:, None] == lax.iota(jnp.int32, 8)[None, :])[:, :, None]
    here = (lax.iota(jnp.int32, depth) == plane)[:, None, None]
    seg_plane = jnp.sum(jnp.where(here, segs, 0), axis=0)
    seg = jnp.sum(jnp.where(picked, seg_plane[None], 0), axis=1).reshape(seq)
    pos = (ids[:, None] * tokens + lax.iota(jnp.int32, tokens)[None, :]).reshape(seq)

    loggam = jnp.log1p(-jnp.exp2(-5.0 - own.astype(F32)))
    gap = pos[:, None] - pos[None, :]
    inside = (gap >= 0) & (seg[:, None] == seg[None, :])
    decay = jnp.where(inside, jnp.exp(jnp.maximum(gap, 0).astype(F32) * loggam), F32(0.0))
    scale = (kq * 2 * depth) ** (-0.5)

    qkv = dot(all_qkv, x_one, ((1,), (1,))).astype(BF16).reshape(depth, -1, seq)
    query = qkv[:, : 2 * kq].reshape(-1, seq)
    keys = qkv[:, 2 * kq : 4 * kq].reshape(-1, seq)
    values = qkv[:, 4 * kq :].reshape(-1, seq)
    raw = dot(query, keys, ((0,), (0,)))
    weights = (raw * scale * decay).astype(BF16)
    retained = dot(values, weights, ((1,), (1,)))
    centered = retained - jnp.mean(retained, axis=0, keepdims=True)
    inv_group = lax.rsqrt(jnp.mean(centered * centered, axis=0, keepdims=True) + EPS_GROUP)
    normed = centered * inv_group
    normed_low = normed.astype(BF16).astype(F32)
    gate = dot(wt_gate, x_one, ((1,), (1,)))
    sigma = jax.nn.sigmoid(gate)
    swish = gate * sigma
    hidden = (swish * normed_low).astype(BF16)
    middle = stream + group_reduce(dot(hidden, wt_out, ((0,), (0,))))

    hat_two, inv_two, norm_two = layernorm(middle, params[2], params[3])
    x_two = group_gather(norm_two)
    pre = dot(wt_up, x_two, ((1,), (1,)))
    act_wide, act_pull = jax.vjp(gelu_exact, pre)
    act = act_wide.astype(BF16)
    grad_act = dot(wt_down, cot, ((1,), (1,)))
    grad_pre = act_pull(grad_act)[0].astype(BF16)
    grad_two = group_reduce(dot(grad_pre, wt_up, ((0,), (0,))))
    ffn = group_reduce(dot(act, wt_down, ((0,), (0,))))
    block_out = from_tokens((middle + ffn).astype(BF16))

    def home(full):
        return lax.psum_scatter(full.astype(BF16), "z", scatter_dimension=0, tiled=True)

    def from_units(mine):
        send = mine.reshape(-1, 4, part).transpose(1, 0, 2)
        return row_exchange(send).reshape(-1, part)

    grad_down = from_units(home(dot(act, cot, ((1,), (0,))))).astype(F32)
    grad_up = from_units(home(dot(grad_pre, x_two, ((1,), (0,))))).T.astype(F32)

    back_two, grad_ffn_gain, grad_ffn_bias = layernorm_back(grad_two, hat_two, inv_two, params[2])
    grad_mid = cot_own.astype(F32) + back_two
    x_mid = group_gather(grad_mid.astype(BF16))

    grad_out_full = dot(hidden, x_mid, ((1,), (0,)))
    grad_hidden = dot(wt_out, x_mid, ((1,), (1,)))
    grad_gate = (grad_hidden * normed_low * (sigma * (1.0 + gate * (1.0 - sigma)))).astype(BF16)
    grad_normed = (grad_hidden * swish).astype(BF16).astype(F32)
    grad_ret = (
        inv_group
        * (
            grad_normed
            - jnp.mean(grad_normed, axis=0, keepdims=True)
            - normed * jnp.mean(grad_normed * normed, axis=0, keepdims=True)
        )
    ).astype(BF16)
    grad_scores = (dot(grad_ret, values, ((0,), (0,))) * decay * scale).astype(BF16)
    grad_q = dot(keys, grad_scores, ((1,), (1,))).astype(BF16)
    grad_k = dot(query, grad_scores, ((1,), (0,))).astype(BF16)
    grad_v = dot(grad_ret, weights, ((1,), (0,))).astype(BF16)
    grad_qkv = jnp.concatenate(
        [
            grad_q.reshape(depth, -1, seq),
            grad_k.reshape(depth, -1, seq),
            grad_v.reshape(depth, -1, seq),
        ],
        axis=1,
    ).reshape(-1, seq)
    grad_one = group_reduce(
        dot(grad_qkv, all_qkv, ((0,), (0,))) + dot(grad_gate, wt_gate, ((0,), (0,)))
    )

    def from_heads(mine, count):
        send = mine.reshape(2, count, 4, part).transpose(2, 0, 1, 3).reshape(8, count, part)
        return lax.all_to_all(send, GROUP, split_axis=0, concat_axis=0, tiled=True)

    home_go = home(
        jnp.concatenate(
            [
                dot(grad_gate, x_one, ((1,), (0,))).reshape(depth, -1, width),
                grad_out_full.reshape(depth, -1, width),
            ],
            axis=1,
        ).reshape(-1, width)
    )
    home_qkv = home(dot(grad_qkv, x_one, ((1,), (0,))))
    go = from_heads(
        jnp.concatenate(
            [home_go[: 2 * kv].reshape(2, kv, width), home_go[2 * kv :].reshape(2, kv, width)],
            axis=1,
        ),
        2 * kv,
    )
    back = from_heads(
        jnp.concatenate(
            [
                home_qkv[: 2 * kq].reshape(2, kq, width),
                home_qkv[2 * kq : 4 * kq].reshape(2, kq, width),
                home_qkv[4 * kq :].reshape(2, kv, width),
            ],
            axis=1,
        ),
        2 * kq + kv,
    )

    def columns(grads, order):
        return dot(grads.reshape(-1, part), order, ((0,), (1,)))

    out_gate = columns(go[:, :kv], order_v)
    out_out = dot(order_v, go[:, kv:].reshape(-1, part), ((1,), (0,)))
    out_query = columns(back[:, :kq], order_q)
    out_key = columns(back[:, kq : 2 * kq], order_q)
    out_value = columns(back[:, 2 * kq :], order_v)

    back_one, grad_attn_gain, grad_attn_bias = layernorm_back(grad_one, hat_one, inv_one, params[0])
    grad_in = from_tokens((grad_mid + back_one).astype(BF16)).astype(F32)
    totals = lax.psum(
        jnp.stack([grad_attn_gain, grad_attn_bias, grad_ffn_gain, grad_ffn_bias]), EVERY
    )
    totals = lax.dynamic_slice_in_dim(totals, lax.axis_index(ROW) * part, part, 1)
    return (
        block_out,
        grad_in,
        out_query,
        out_key,
        out_value,
        out_gate,
        out_out,
        grad_up,
        grad_down,
        totals[0],
        totals[1],
        totals[2],
        totals[3],
    )


def solution(mesh):
    rows, cols = mesh.devices.shape
    fine = Mesh(mesh.devices.reshape(rows // 2, 2, cols // 2, 2), ("x", "k", "z", "y"))
    row, col = ("x", "k"), ("z", "y")
    tok, unit = P(col, row), P(row, col)
    return jax.shard_map(
        body,
        mesh=fine,
        in_specs=(tok, tok, P(row), unit, unit, unit, unit, tok, unit, tok)
        + (P(row),) * 4,
        out_specs=(tok, tok, unit, unit, unit, unit, tok, unit, tok) + (P(row),) * 4,
        check_vma=False,
    )
```

```python
import jax
import jax.numpy as jnp
from jax import lax
from jax.sharding import Mesh
from jax.sharding import PartitionSpec as P

HEADS = 8
EPS_NORM = 1e-05
EPS_GROUP = 0.25

ROW = ("x", "k")
GROUP = ("x", "k", "y")
EVERY = ("x", "k", "z", "y")
F32 = jnp.float32
BF16 = jnp.bfloat16


def dot(left, right, over):
    return lax.dot_general(left, right, (over, ((), ())), preferred_element_type=F32)


def swap(value, mask):
    return lax.ppermute(value, GROUP, [(i, i ^ mask) for i in range(8)])


def group_gather(part):
    near = [part, swap(part, 1), swap(part, 4), swap(part, 5)]
    far = [swap(block, 2) for block in near]
    return jnp.concatenate(near[:2] + far[:2] + near[2:] + far[2:], axis=0)


def group_reduce(total):
    height = total.shape[0] // 8
    half = height // 2

    def pair(j):
        kept = total[j * height : (j + 1) * height]
        sent = total[(j + 2) * height : (j + 3) * height].astype(BF16)
        return kept + swap(sent, 2).astype(F32)

    across, over_x, over_y, own = pair(5).astype(BF16), pair(4), pair(1), pair(0)
    top, low = swap(across[:half], 1).astype(F32), swap(across[half:], 4).astype(F32)
    over_x = jnp.concatenate([over_x[:half] + top, over_x[half:]], axis=0).astype(BF16)
    over_y = jnp.concatenate([over_y[:half], over_y[half:] + low], axis=0).astype(BF16)
    return own + swap(over_x, 4).astype(F32) + swap(over_y, 1).astype(F32)


def after(value, *others):
    return lax.optimization_barrier((value,) + others)[0]


def total_over_all(value):
    for mask in (2, 1, 4):
        value = value + swap(value, mask)
    depth = lax.axis_size("z")
    if depth > 4:
        return lax.psum(value, "z")
    own = value
    for step in range(1, depth):
        value = value + lax.ppermute(own, "z", [(i, (i + step) % depth) for i in range(depth)])
    return value


def row_gather(value):
    got = [value, swap(value, 2), swap(value, 4), swap(value, 6)]
    own = lax.axis_index(ROW)
    rows = []
    for i in range(4):
        picks = [jnp.where((own ^ j) == i, got[j], 0.0) for j in range(4)]
        rows.append(picks[0] + picks[1] + picks[2] + picks[3])
    return jnp.stack(rows)


def row_exchange(parts):
    return lax.all_to_all(parts, ROW, split_axis=0, concat_axis=0, tiled=True)


def to_wide(*parts):
    height, width = parts[0].shape
    moved = row_exchange(jnp.stack([p.reshape(4, -1, width) for p in parts], axis=1))
    moved = moved.transpose(1, 2, 0, 3).reshape(len(parts), height // 4, 4 * width)
    return [moved[i] for i in range(len(parts))]


def from_tokens(part):
    tokens, width = part.shape
    moved = row_exchange(part.reshape(tokens, 4, width // 4).transpose(1, 0, 2))
    return moved.reshape(4 * tokens, width // 4)


def head_order(count):
    units = count // HEADS
    j = lax.iota(jnp.int32, count)
    target = (j % HEADS) * units + j // HEADS
    return (target[:, None] == lax.iota(jnp.int32, count)[None, :]).astype(BF16)


def layernorm(value, gain, bias):
    mean = jnp.mean(value, axis=1, keepdims=True)
    centered = value - mean
    inverse = lax.rsqrt(jnp.mean(centered * centered, axis=1, keepdims=True) + EPS_NORM)
    hat = centered * inverse
    return hat, inverse, (hat * gain + bias).astype(BF16)


def layernorm_back(grad, hat, inverse, gain):
    scaled = grad * gain
    first = jnp.mean(scaled, axis=1, keepdims=True)
    second = jnp.mean(scaled * hat, axis=1, keepdims=True)
    return (
        inverse * (scaled - first - hat * second),
        jnp.sum(grad * hat, axis=0),
        jnp.sum(grad, axis=0),
    )


def gelu_exact(value):
    return jax.nn.gelu(value, approximate=False)


def body(
    block_in,
    cotangent,
    segments,
    w_query,
    w_key,
    w_value,
    w_gate,
    w_out,
    w_up,
    w_down,
    retention_norm_gain,
    retention_norm_bias,
    feedforward_norm_gain,
    feedforward_norm_bias,
):
    depth = lax.axis_size("z")
    part = block_in.shape[1]
    width = 4 * part
    own = lax.axis_index(GROUP)
    plane = lax.axis_index("z")
    tokens = block_in.shape[0] // 4
    seq = 8 * tokens

    kq = w_query.shape[1] // HEADS
    kv = w_value.shape[1] // HEADS
    order_q = head_order(w_query.shape[1])
    order_v = head_order(w_value.shape[1])

    def by_head(weight, order):
        return dot(order, weight, ((0,), (1,))).astype(BF16).reshape(HEADS, -1, part)

    def to_heads(send):
        got = lax.all_to_all(send, GROUP, split_axis=0, concat_axis=0, tiled=True)
        got = got.reshape(4, 2, send.shape[1], part).transpose(1, 2, 0, 3)
        return got.reshape(2, send.shape[1], width)

    def planes(mine):
        return lax.all_gather(mine, "z", axis=0, tiled=True)

    got_qkv = to_heads(
        jnp.concatenate(
            [by_head(w_query, order_q), by_head(w_key, order_q), by_head(w_value, order_v)], axis=1
        )
    )
    mine_qkv = jnp.concatenate(
        [
            got_qkv[:, :kq].reshape(2 * kq, width),
            got_qkv[:, kq : 2 * kq].reshape(2 * kq, width),
            got_qkv[:, 2 * kq :].reshape(2 * kv, width),
        ],
        axis=0,
    )
    all_qkv = planes(mine_qkv)
    send_go = jnp.concatenate(
        [
            by_head(w_gate, order_v),
            dot(order_v, w_out, ((0,), (0,))).astype(BF16).reshape(HEADS, -1, part),
        ],
        axis=1,
    )
    got_go = to_heads(after(send_go, mine_qkv))
    mine_go = jnp.concatenate(
        [got_go[:, :kv].reshape(2 * kv, width), got_go[:, kv:].reshape(2 * kv, width)], axis=0
    )
    all_go = planes(mine_go).reshape(depth, 4 * kv, width)

    small = jnp.concatenate(
        [
            retention_norm_gain,
            retention_norm_bias,
            feedforward_norm_gain,
            feedforward_norm_bias,
            segments.astype(F32),
        ]
    )
    small = row_gather(after(small, mine_qkv))
    params = small[:, : 4 * part].reshape(4, 4, part).transpose(1, 0, 2).reshape(4, width)
    segs = small[:, 4 * part :].astype(jnp.int32).reshape(depth, 8, tokens)
    block_in, cotangent = after(block_in, got_go), after(cotangent, got_go)
    stream_low, cot_own = to_wide(block_in, cotangent)
    mine_up, mine_down = to_wide(after(w_up, stream_low).T, after(w_down, stream_low))
    wt_up = planes(after(mine_up, mine_go))
    wt_down = planes(after(mine_down, mine_go))
    stream = stream_low.astype(F32)
    hat_one, inv_one, norm_one = layernorm(stream, params[0], params[1])
    x_one = group_gather(norm_one)

    ids = lax.iota(jnp.int32, 8) ^ own
    ids = (ids % 2) * 4 + ids // 2
    picked = (ids[:, None] == lax.iota(jnp.int32, 8)[None, :])[:, :, None]
    here = (lax.iota(jnp.int32, depth) == plane)[:, None, None]
    seg_plane = jnp.sum(jnp.where(here, segs, 0), axis=0)
    seg = jnp.sum(jnp.where(picked, seg_plane[None], 0), axis=1).reshape(seq)
    pos = (ids[:, None] * tokens + lax.iota(jnp.int32, tokens)[None, :]).reshape(seq)

    loggam = jnp.log1p(-jnp.exp2(-5.0 - own.astype(F32)))
    gap = pos[:, None] - pos[None, :]
    inside = (gap >= 0) & (seg[:, None] == seg[None, :])
    decay = jnp.where(inside, jnp.exp(jnp.maximum(gap, 0).astype(F32) * loggam), F32(0.0))
    scale = (kq * 2 * depth) ** (-0.5)

    x_one = after(x_one, mine_up, mine_down)
    qkv = dot(all_qkv, x_one, ((1,), (1,))).astype(BF16).reshape(depth, -1, seq)
    query = qkv[:, : 2 * kq].reshape(-1, seq)
    keys = qkv[:, 2 * kq : 4 * kq].reshape(-1, seq)
    values = qkv[:, 4 * kq :].reshape(-1, seq)
    raw = dot(query, keys, ((0,), (0,)))
    weights = (raw * scale * decay).astype(BF16)
    retained = dot(values, weights, ((1,), (1,)))
    centered = retained - jnp.mean(retained, axis=0, keepdims=True)
    inv_group = lax.rsqrt(jnp.mean(centered * centered, axis=0, keepdims=True) + EPS_GROUP)
    normed = centered * inv_group
    normed_low = normed.astype(BF16).astype(F32)
    cot = group_gather(after(cot_own, x_one))
    retained = after(retained, cot)
    wt_gate = all_go[:, : 2 * kv].reshape(-1, width)
    wt_out = all_go[:, 2 * kv :].reshape(-1, width)
    gate = dot(wt_gate, after(x_one, normed), ((1,), (1,)))
    sigma = jax.nn.sigmoid(gate)
    swish = gate * sigma
    hidden = (swish * normed_low).astype(BF16)
    attn = dot(hidden, wt_out, ((0,), (0,)))
    middle = stream + group_reduce(attn)

    hat_two, inv_two, norm_two = layernorm(middle, params[2], params[3])
    x_two = group_gather(norm_two)
    grad_act = dot(wt_down, cot, ((1,), (1,)))
    pre = dot(wt_up, x_two, ((1,), (1,)))
    act_wide, act_pull = jax.vjp(gelu_exact, pre)
    act = act_wide.astype(BF16)
    grad_pre = act_pull(grad_act)[0].astype(BF16)
    two_part = dot(grad_pre, wt_up, ((0,), (0,)))
    grad_two = group_reduce(two_part)

    def home(*fulls):
        fulls = [f.astype(BF16).reshape(depth, -1, width) for f in fulls]
        full = jnp.concatenate(fulls, axis=1).reshape(-1, width)
        return lax.psum_scatter(full, "z", scatter_dimension=0, tiled=True)

    def from_units(mine):
        send = mine.reshape(-1, 4, part).transpose(1, 0, 2)
        return row_exchange(send).reshape(-1, part)

    home_ud = home(dot(act, cot, ((1,), (0,))), dot(grad_pre, x_two, ((1,), (0,))))

    back_two, grad_ffn_gain, grad_ffn_bias = layernorm_back(grad_two, hat_two, inv_two, params[2])
    grad_mid = cot_own.astype(F32) + back_two
    x_mid = group_gather(grad_mid.astype(BF16))

    grad_hidden = dot(wt_out, x_mid, ((1,), (1,)))
    grad_gate = (grad_hidden * normed_low * (sigma * (1.0 + gate * (1.0 - sigma)))).astype(BF16)
    home_go = home(dot(grad_gate, x_one, ((1,), (0,))), dot(hidden, x_mid, ((1,), (0,))))
    grad_normed = (grad_hidden * swish).astype(BF16).astype(F32)
    grad_ret = (
        inv_group
        * (
            grad_normed
            - jnp.mean(grad_normed, axis=0, keepdims=True)
            - normed * jnp.mean(grad_normed * normed, axis=0, keepdims=True)
        )
    ).astype(BF16)
    grad_scores = (dot(grad_ret, values, ((0,), (0,))) * decay * scale).astype(BF16)
    grad_q = dot(keys, grad_scores, ((1,), (1,))).astype(BF16)
    grad_k = dot(query, grad_scores, ((1,), (0,))).astype(BF16)
    grad_v = dot(grad_ret, weights, ((1,), (0,))).astype(BF16)
    grad_qkv = jnp.concatenate(
        [
            grad_q.reshape(depth, -1, seq),
            grad_k.reshape(depth, -1, seq),
            grad_v.reshape(depth, -1, seq),
        ],
        axis=1,
    ).reshape(-1, seq)
    full_qkv = dot(grad_qkv, x_one, ((1,), (0,))).astype(BF16)
    home_qkv = home(full_qkv)
    grad_qkv, grad_gate = after(grad_qkv, full_qkv), after(grad_gate, full_qkv)
    grad_one = group_reduce(
        dot(grad_qkv, all_qkv, ((0,), (0,))) + dot(grad_gate, wt_gate, ((0,), (0,)))
    )
    ffn = group_reduce(dot(after(act, grad_qkv), wt_down, ((0,), (0,))))
    block_out = from_tokens((middle + ffn).astype(BF16))

    def from_heads(mine, count):
        send = mine.reshape(2, count, 4, part).transpose(2, 0, 1, 3).reshape(8, count, part)
        return lax.all_to_all(send, GROUP, split_axis=0, concat_axis=0, tiled=True)

    def columns(grads, order):
        return dot(grads.reshape(-1, part), order, ((0,), (1,)))

    back_one, grad_attn_gain, grad_attn_bias = layernorm_back(grad_one, hat_one, inv_one, params[0])
    grad_in = from_tokens((grad_mid + back_one).astype(BF16)).astype(F32)
    totals = total_over_all(
        jnp.stack([grad_attn_gain, grad_attn_bias, grad_ffn_gain, grad_ffn_bias])
    )
    totals = lax.dynamic_slice_in_dim(totals, lax.axis_index(ROW) * part, part, 1)

    home_ud = after(home_ud, grad_one)
    half = home_ud.shape[0] // 2
    grad_down = from_units(home_ud[:half]).astype(F32)
    grad_up = from_units(home_ud[half:]).T.astype(F32)
    home_go = after(home_go, grad_in, grad_down, grad_up, block_out)
    go = from_heads(
        jnp.concatenate(
            [home_go[: 2 * kv].reshape(2, kv, width), home_go[2 * kv :].reshape(2, kv, width)],
            axis=1,
        ),
        2 * kv,
    )
    home_qkv = after(home_qkv, go, totals)
    back = from_heads(
        jnp.concatenate(
            [
                home_qkv[: 2 * kq].reshape(2, kq, width),
                home_qkv[2 * kq : 4 * kq].reshape(2, kq, width),
                home_qkv[4 * kq :].reshape(2, kv, width),
            ],
            axis=1,
        ),
        2 * kq + kv,
    )
    out_gate = columns(go[:, :kv], order_v)
    out_out = dot(order_v, go[:, kv:].reshape(-1, part), ((1,), (0,)))
    out_query = columns(back[:, :kq], order_q)
    out_key = columns(back[:, kq : 2 * kq], order_q)
    out_value = columns(back[:, 2 * kq :], order_v)
    return (
        block_out,
        grad_in,
        out_query,
        out_key,
        out_value,
        out_gate,
        out_out,
        grad_up,
        grad_down,
        totals[0],
        totals[1],
        totals[2],
        totals[3],
    )


def solution(mesh):
    rows, cols = mesh.devices.shape
    fine = Mesh(mesh.devices.reshape(rows // 2, 2, cols // 2, 2), ("x", "k", "z", "y"))
    row, col = ("x", "k"), ("z", "y")
    tok, unit = P(col, row), P(row, col)
    return jax.shard_map(
        body,
        mesh=fine,
        in_specs=(tok, tok, P(row), unit, unit, unit, unit, tok, unit, tok)
        + (P(row),) * 4,
        out_specs=(tok, tok, unit, unit, unit, unit, tok, unit, tok) + (P(row),) * 4,
        check_vma=False,
    )
```

```python
import functools
import math

import jax
import jax.numpy as jnp
import numpy as np
from jax import lax
from jax.experimental import pallas as pl
from jax.experimental.pallas import tpu as pltpu
from jax.sharding import Mesh
from jax.sharding import PartitionSpec as P

HEADS = 8
EPS_NORM = 1e-05
EPS_GROUP = 0.25

ROW = ("x", "k")
GROUP = ("x", "k", "y")
EVERY = ("x", "k", "z", "y")
F32 = jnp.float32
BF16 = jnp.bfloat16


def dot(left, right, over):
    return lax.dot_general(left, right, (over, ((), ())), preferred_element_type=F32)


def swap(value, mask):
    return lax.ppermute(value, GROUP, [(i, i ^ mask) for i in range(8)])


def group_gather(part, *others):
    near = [part, swap(part, 1), swap(part, 4), swap(part, 5)]
    far = [swap(after(block, *others), 2) for block in near]
    return near[:2] + far[:2] + near[2:] + far[2:]


def reduce_pairs(total):
    height = total.shape[0] // 8

    def pair(j):
        kept = total[j * height : (j + 1) * height]
        return kept.astype(F32) + swap(total[(j + 2) * height : (j + 3) * height], 2).astype(F32)

    return pair(5).astype(BF16), pair(4), pair(1), pair(0)


def reduce_relay(state):
    across, over_x, over_y, own = state
    half = across.shape[0] // 2
    top, low = swap(across[:half], 1).astype(F32), swap(across[half:], 4).astype(F32)
    over_x = jnp.concatenate([over_x[:half] + top, over_x[half:]], axis=0).astype(BF16)
    over_y = jnp.concatenate([over_y[:half], over_y[half:] + low], axis=0).astype(BF16)
    return over_x, over_y, own


def reduce_last(state):
    over_x, over_y, own = state
    return own + swap(over_x, 4).astype(F32) + swap(over_y, 1).astype(F32)


def group_reduce(total):
    return reduce_last(reduce_relay(reduce_pairs(total)))


def after(value, *others):
    return lax.optimization_barrier((value,) + others)[0]


def total_over_all(value):
    value = value + swap(value, 2)
    value = value + swap(value, 1) + swap(value, 4) + swap(value, 5)
    depth = lax.axis_size("z")
    if depth > 4:
        return lax.psum(value, "z")
    own = value
    for step in range(1, depth):
        value = value + lax.ppermute(own, "z", [(i, (i + step) % depth) for i in range(depth)])
    return value


def row_gather(value):
    got = [value, swap(value, 2), swap(value, 4), swap(value, 6)]
    own = lax.axis_index(ROW)
    rows = []
    for i in range(4):
        picks = [jnp.where((own ^ j) == i, got[j], 0.0) for j in range(4)]
        rows.append(picks[0] + picks[1] + picks[2] + picks[3])
    return jnp.stack(rows)


def row_exchange(parts):
    return lax.all_to_all(parts, ROW, split_axis=0, concat_axis=0, tiled=True)


def to_wide(*parts):
    height, width = parts[0].shape
    moved = row_exchange(jnp.stack([p.reshape(4, -1, width) for p in parts], axis=1))
    moved = moved.transpose(1, 2, 0, 3).reshape(len(parts), height // 4, 4 * width)
    return [moved[i] for i in range(len(parts))]


def from_wide(*parts):
    height, width = parts[0].shape
    moved = row_exchange(
        jnp.stack(parts).reshape(len(parts), height, 4, width // 4).transpose(2, 0, 1, 3)
    )
    moved = moved.transpose(1, 0, 2, 3).reshape(len(parts), 4 * height, width // 4)
    return [moved[i] for i in range(len(parts))]


def head_order(count):
    units = count // HEADS
    j = lax.iota(jnp.int32, count)
    target = (j % HEADS) * units + j // HEADS
    return (target[:, None] == lax.iota(jnp.int32, count)[None, :]).astype(BF16)


def layernorm(value, gain, bias):
    mean = jnp.mean(value, axis=1, keepdims=True)
    centered = value - mean
    inverse = lax.rsqrt(jnp.mean(centered * centered, axis=1, keepdims=True) + EPS_NORM)
    hat = centered * inverse
    return hat, inverse, (hat * gain + bias).astype(BF16)


def layernorm_back(grad, hat, inverse, gain):
    scaled = grad * gain
    first = jnp.mean(scaled, axis=1, keepdims=True)
    second = jnp.mean(scaled * hat, axis=1, keepdims=True)
    return (
        inverse * (scaled - first - hat * second),
        jnp.sum(grad * hat, axis=0),
        jnp.sum(grad, axis=0),
    )


TILE = 256
WIDE = 512
LIMIT = 58 * 1024 * 1024


def spans(total, tile, step):
    def once(i, carry):
        step(pl.ds(pl.multiple_of(i * tile, tile), tile))
        return carry

    lax.fori_loop(0, total // tile, once, 0)


def kernel_call(body, outs, scratch, flops, *args, copies=0):
    moved = sum(a.size * a.dtype.itemsize for a in args)
    moved += sum(math.prod(shape) * jnp.dtype(kind).itemsize for shape, kind in outs)
    whole = pl.BlockSpec(memory_space=pl.ANY if copies else pltpu.VMEM)
    return pl.pallas_call(
        body,
        out_shape=[jax.ShapeDtypeStruct(shape, kind) for shape, kind in outs],
        in_specs=[whole] * len(args),
        out_specs=[whole] * len(outs),
        scratch_shapes=[pltpu.VMEM(shape, kind) for shape, kind in scratch]
        + [pltpu.SemaphoreType.DMA((copies,))] * bool(copies),
        compiler_params=pltpu.CompilerParams(vmem_limit_bytes=LIMIT),
        cost_estimate=pl.CostEstimate(flops=flops, bytes_accessed=moved, transcendentals=0),
    )(*args)


def unpack(source, first, second, depth):
    half = source.shape[0] // (2 * depth)
    for i in range(depth):
        at = 2 * i * half
        if first is not None:
            first[i * half : (i + 1) * half, :] = source[at : at + half, :]
        if second is not None:
            second[i * half : (i + 1) * half, :] = source[at + half : at + 2 * half, :]


def pack(target, columns, first, second, depth):
    half = first.shape[0] // depth
    for i in range(depth):
        at = 2 * i * half
        target[at : at + half, columns] = first[i * half : (i + 1) * half]
        target[at + half : at + 2 * half, columns] = second[i * half : (i + 1) * half]


def decayed(raw, spot, segs, grow, fall, rows):
    inside = (spot[0][rows, :] >= spot[1][...]) & (segs[0][rows, :] == segs[1][...])
    return jnp.where(inside, raw * (grow[rows, :] * fall[...]), 0.0).astype(BF16)


def retention_forward(depth, w, x, pc, pr, sc, sr, grow, fall, q, k, v, weights, normed, inv):
    seq = x.shape[0]
    part = q.shape[0] // depth
    width = v.shape[0] // depth
    group = 2 * part + width

    def project(at):
        out = dot(w[...], x[at, :], ((1,), (1,))).astype(BF16)
        for i in range(depth):
            z = i * group
            q[i * part : (i + 1) * part, at] = out[z : z + part]
            k[i * part : (i + 1) * part, at] = out[z + part : z + 2 * part]
            v[i * width : (i + 1) * width, at] = out[z + 2 * part : z + group]

    def attend(at):
        raw = dot(q[:, at], k[...], ((0,), (0,)))
        low = decayed(raw, (pc, pr), (sc, sr), grow, fall, at)
        weights[at, :] = low
        kept = dot(v[...], low, ((1,), (1,)))
        centered = kept - jnp.mean(kept, axis=0, keepdims=True)
        scale = lax.rsqrt(jnp.mean(centered * centered, axis=0, keepdims=True) + EPS_GROUP)
        normed[:, at] = centered * scale
        inv[:, at] = scale

    spans(seq, TILE, project)
    spans(seq, TILE, attend)


def gated_forward(depth, w, x, normed, gate, hidden, out, wg, wo):
    unpack(w, wg, wo, depth)

    def step(at):
        g = dot(wg[...], x[at, :], ((1,), (1,)))
        gate[:, at] = g
        low = normed[:, at].astype(BF16).astype(F32)
        h = (g * jax.nn.sigmoid(g) * low).astype(BF16)
        hidden[:, at] = h
        out[at, :] = dot(h, wo[...], ((0,), (0,))).astype(BF16)

    spans(x.shape[0], TILE, step)


class Mover:
    def __init__(self, semaphores):
        self.semaphores = semaphores
        self.count = 0

    def start(self, source, target):
        copy = pltpu.make_async_copy(source, target, self.semaphores.at[self.count])
        self.count += 1
        copy.start()
        return copy

    def rows(self, sources, target):
        height = sources[0].shape[0]
        return [
            self.start(source, target.at[pl.ds(i * height, height)])
            for i, source in enumerate(sources)
        ]

    def kind(self, source, target, which, depth):
        half = (source if which[0] == "from" else target).shape[0] // (2 * depth)
        moved = []
        for i in range(depth):
            mixed = pl.ds((2 * i + which[1]) * half, half)
            plain = pl.ds(i * half, half)
            if which[0] == "from":
                moved.append(self.start(source.at[mixed], target.at[plain]))
            else:
                moved.append(self.start(source.at[plain], target.at[mixed]))
        return moved


def wait(copies):
    for copy in copies:
        copy.wait()


def feedforward(depth, w, *refs):
    x_blocks, cot_blocks = refs[:8], refs[8:16]
    act_out, back_out, grads_out = refs[16:19]
    wu, wd, x, cot, act, gp, back, gu, gd, semaphores = refs[19:]
    move = Mover(semaphores)
    seq, rows = x.shape[0], x_blocks[0].shape[0]
    weights = move.kind(w, wu, ("from", 0), depth) + move.kind(w, wd, ("from", 1), depth)
    x_copies, cot_copies = move.rows(x_blocks, x), move.rows(cot_blocks, cot)
    wait(weights)
    for tile in range(seq // TILE):
        mine = slice(tile * TILE // rows, (tile + 1) * TILE // rows)
        wait(x_copies[mine] + cot_copies[mine])
        at = pl.ds(tile * TILE, TILE)
        pre = dot(wu[...], x[at, :], ((1,), (1,)))
        grad = dot(wd[...], cot[at, :], ((1,), (1,)))
        half = 0.5 * (1.0 + lax.erf(pre * np.float32(0.5**0.5)))
        act[:, at] = (pre * half).astype(BF16)
        bell = jnp.exp(-0.5 * pre * pre) * np.float32((2 * math.pi) ** -0.5)
        gp[:, at] = (grad * (half + pre * bell)).astype(BF16)
    sent = [move.start(act, act_out)]

    def up_step(at):
        gu[:, at] = dot(gp[...], x[:, at], ((1,), (0,))).astype(BF16)

    def down_step(at):
        gd[:, at] = dot(act[...], cot[:, at], ((1,), (0,))).astype(BF16)

    spans(x.shape[1], WIDE, up_step)
    sent += move.kind(gu, grads_out, ("to", 0), depth)
    spans(x.shape[1], WIDE, down_step)
    sent += move.kind(gd, grads_out, ("to", 1), depth)
    for tile in range(seq // TILE):
        at = pl.ds(tile * TILE, TILE)
        back[at, :] = dot(gp[:, at], wu[...], ((0,), (0,))).astype(BF16)
        sent.append(move.start(back.at[at], back_out.at[at]))
    wait(sent)


def down_forward(depth, w, act, out, wd):
    unpack(w, None, wd, depth)

    def step(at):
        out[at, :] = dot(act[:, at], wd[...], ((0,), (0,))).astype(BF16)

    spans(act.shape[1], TILE, step)


def gated_backward(depth, w, x_in, *refs):
    mid_blocks = refs[:8]
    gate_in, normed_in, inv_in, hidden_in, ggate_out, gret_out, grads_out = refs[8:15]
    wo, x, mid, gate, normed, inv, hidden, ggate, gret, gg, go, semaphores = refs[15:]
    move = Mover(semaphores)
    seq, rows = x.shape[0], mid_blocks[0].shape[0]
    first = move.kind(w, wo, ("from", 1), depth)
    mid_copies = move.rows(mid_blocks[:2], mid.at[pl.ds(0, 2 * rows)])
    first += [move.start(inv_in, inv), move.start(gate_in, gate), move.start(normed_in, normed)]
    mid_copies += move.rows(mid_blocks[2:], mid.at[pl.ds(2 * rows, seq - 2 * rows)])
    late = [move.start(x_in, x), move.start(hidden_in, hidden)]
    wait(first)
    for tile in range(seq // TILE):
        wait(mid_copies[tile * TILE // rows : (tile + 1) * TILE // rows])
        at = pl.ds(tile * TILE, TILE)
        up = dot(wo[...], mid[at, :], ((1,), (1,)))
        g = gate[:, at]
        s = jax.nn.sigmoid(g)
        full = normed[:, at]
        low = full.astype(BF16).astype(F32)
        ggate[:, at] = (up * low * (s * (1.0 + g * (1.0 - s)))).astype(BF16)
        gn = (up * (g * s)).astype(BF16).astype(F32)
        mean = jnp.mean(gn, axis=0, keepdims=True)
        slope = jnp.mean(gn * full, axis=0, keepdims=True)
        gret[:, at] = (inv[:, at] * (gn - mean - full * slope)).astype(BF16)
    sent = [move.start(ggate, ggate_out), move.start(gret, gret_out)]
    wait(late)

    def gate_step(at):
        gg[:, at] = dot(ggate[...], x[:, at], ((1,), (0,))).astype(BF16)

    def out_step(at):
        go[:, at] = dot(hidden[...], mid[:, at], ((1,), (0,))).astype(BF16)

    spans(x.shape[1], WIDE, gate_step)
    sent += move.kind(gg, grads_out, ("to", 0), depth)
    spans(x.shape[1], WIDE, out_step)
    sent += move.kind(go, grads_out, ("to", 1), depth)
    wait(sent)


def retention_backward(
    depth, q, k, v, weights, gret, x, pc, pr, sc, sr, grow, fall, packed, grads, scores
):
    seq = x.shape[0]
    part = q.shape[0] // depth
    width = v.shape[0] // depth
    group = 2 * part + width

    def place(value, at, offset, height):
        for i in range(depth):
            z = i * group + offset
            packed[z : z + height, at] = value[i * height : (i + 1) * height]

    def query_step(at):
        raw = dot(gret[:, at], v[...], ((0,), (0,)))
        low = decayed(raw, (pc, pr), (sc, sr), grow, fall, at)
        scores[at, :] = low
        place(dot(k[...], low, ((1,), (1,))).astype(BF16), at, 0, part)

    def key_step(at):
        place(dot(q[...], scores[:, at], ((1,), (0,))).astype(BF16), at, part, part)
        place(dot(gret[...], weights[:, at], ((1,), (0,))).astype(BF16), at, 2 * part, width)

    def grad_step(at):
        grads[:, at] = dot(packed[...], x[:, at], ((1,), (0,))).astype(BF16)

    spans(seq, TILE, query_step)
    spans(seq, TILE, key_step)
    spans(x.shape[1], WIDE, grad_step)


def input_backward(depth, packed, w, ggate, wgo, out, wg):
    unpack(wgo, wg, None, depth)

    def step(at):
        total = dot(packed[:, at], w[...], ((0,), (0,)))
        out[at, :] = (total + dot(ggate[:, at], wg[...], ((0,), (0,)))).astype(BF16)

    spans(packed.shape[1], TILE, step)


def body(
    block_in,
    cotangent,
    segments,
    w_query,
    w_key,
    w_value,
    w_gate,
    w_out,
    w_up,
    w_down,
    retention_norm_gain,
    retention_norm_bias,
    feedforward_norm_gain,
    feedforward_norm_bias,
):
    depth = lax.axis_size("z")
    part = block_in.shape[1]
    width = 4 * part
    own = lax.axis_index(GROUP)
    plane = lax.axis_index("z")
    tokens = block_in.shape[0] // 4
    seq = 8 * tokens

    kq = w_query.shape[1] // HEADS
    kv = w_value.shape[1] // HEADS
    order_q = head_order(w_query.shape[1])
    order_v = head_order(w_value.shape[1])

    def by_head(weight, order):
        return dot(order, weight, ((0,), (1,))).astype(BF16).reshape(HEADS, -1, part)

    def to_heads(send):
        got = lax.all_to_all(send, GROUP, split_axis=0, concat_axis=0, tiled=True)
        got = got.reshape(4, 2, send.shape[1], part).transpose(1, 2, 0, 3)
        return got.reshape(2, send.shape[1], width)

    split = 2 if kq % 16 == 0 else 1
    blocks = depth * split

    def regroup(rows, *counts):
        if split == 2:
            return rows.reshape(-1, width)
        cuts = np.cumsum((0,) + counts)
        return jnp.concatenate(
            [rows[:, cuts[i] : cuts[i + 1]].reshape(-1, width) for i in range(len(counts))]
        )

    def ungroup(rows, *counts):
        if split == 2:
            return rows.reshape(2, -1, width)
        cuts = 2 * np.cumsum((0,) + counts)
        return jnp.concatenate(
            [rows[cuts[i] : cuts[i + 1]].reshape(2, -1, width) for i in range(len(counts))], axis=1
        )

    def planes(mine):
        return lax.all_gather(mine, "z", axis=0, tiled=True)

    got_qkv = to_heads(
        jnp.concatenate(
            [by_head(w_query, order_q), by_head(w_key, order_q), by_head(w_value, order_v)], axis=1
        )
    )
    mine_qkv = regroup(got_qkv, kq, kq, kv)
    all_qkv = planes(mine_qkv)
    send_go = jnp.concatenate(
        [
            by_head(w_gate, order_v),
            dot(order_v, w_out, ((0,), (0,))).astype(BF16).reshape(HEADS, -1, part),
        ],
        axis=1,
    )
    got_go = to_heads(after(send_go, mine_qkv))
    mine_go = regroup(got_go, kv, kv)
    all_go = planes(mine_go)

    small = jnp.concatenate(
        [
            retention_norm_gain,
            retention_norm_bias,
            feedforward_norm_gain,
            feedforward_norm_bias,
            segments.astype(F32),
        ]
    )
    small = row_gather(after(small, mine_qkv))
    params = small[:, : 4 * part].reshape(4, 4, part).transpose(1, 0, 2).reshape(4, width)
    segs = small[:, 4 * part :].astype(jnp.int32).reshape(depth, 8, tokens)
    block_in, cotangent = after(block_in, got_go), after(cotangent, got_go)
    stream_low, cot_own = to_wide(block_in, cotangent)
    mine_up, mine_down = to_wide(after(w_up, stream_low).T, after(w_down, stream_low))
    all_ud = planes(after(jnp.concatenate([mine_up, mine_down], axis=0), mine_go))
    stream = stream_low.astype(F32)
    hat_one, inv_one, norm_one = layernorm(stream, params[0], params[1])
    x_one = jnp.concatenate(group_gather(norm_one), axis=0)

    ids = lax.iota(jnp.int32, 8) ^ own
    ids = (ids % 2) * 4 + ids // 2
    picked = (ids[:, None] == lax.iota(jnp.int32, 8)[None, :])[:, :, None]
    here = (lax.iota(jnp.int32, depth) == plane)[:, None, None]
    seg_plane = jnp.sum(jnp.where(here, segs, 0), axis=0)
    seg = jnp.sum(jnp.where(picked, seg_plane[None], 0), axis=1).reshape(seq)
    pos = (ids[:, None] * tokens + lax.iota(jnp.int32, tokens)[None, :]).reshape(seq)

    loggam = jnp.log1p(-jnp.exp2(-5.0 - own.astype(F32)))
    lag = (pos - seq // 2).astype(F32) * loggam
    grow = jnp.exp(lag) * np.float32((kq * 2 * depth) ** (-0.5))
    where = (pos[:, None], pos[None, :], seg[:, None], seg[None, :])
    where = where + (grow[:, None], jnp.exp(-lag)[None, :])

    x_one = after(x_one, mine_up, mine_down)
    keys_all, values_all = kq * 2 * depth, kv * 2 * depth
    square = 2 * seq * seq
    query, keys, values, weights, normed, inv_group = kernel_call(
        functools.partial(retention_forward, blocks),
        [
            ((keys_all, seq), BF16),
            ((keys_all, seq), BF16),
            ((values_all, seq), BF16),
            ((seq, seq), BF16),
            ((values_all, seq), F32),
            ((1, seq), F32),
        ],
        [],
        2 * seq * width * all_qkv.shape[0] + square * (keys_all + values_all),
        all_qkv,
        x_one,
        *where,
    )
    cot = group_gather(after(cot_own, x_one))
    wide = 2 * seq * width * values_all
    gate, hidden, attn = kernel_call(
        functools.partial(gated_forward, blocks),
        [((values_all, seq), F32), ((values_all, seq), BF16), ((seq, width), BF16)],
        [((values_all, width), BF16), ((values_all, width), BF16)],
        2 * wide,
        all_go,
        x_one,
        after(normed, cot),
    )
    middle = stream + group_reduce(attn)

    hat_two, inv_two, norm_two = layernorm(middle, params[2], params[3])
    x_two = group_gather(norm_two, all_ud)
    hidden_all = all_ud.shape[0] // 2
    wide_ff = 2 * seq * width * hidden_all
    narrow, broad = ((hidden_all, seq), BF16), ((hidden_all, width), BF16)
    tall = ((seq, width), BF16)
    act, two_part, full_ud = kernel_call(
        functools.partial(feedforward, depth),
        [narrow, tall, (all_ud.shape, BF16)],
        [broad, broad, tall, tall, narrow, narrow, tall, broad, broad],
        5 * wide_ff,
        all_ud,
        *x_two,
        *cot,
        copies=4 * depth + 17 + seq // TILE,
    )
    grad_two = group_reduce(two_part)

    def home(full):
        return lax.psum_scatter(full, "z", scatter_dimension=0, tiled=True)

    def from_units(mine):
        send = mine.reshape(-1, 4, part).transpose(1, 0, 2)
        return row_exchange(send).reshape(-1, part)

    home_ud = home(full_ud)

    back_two, grad_ffn_gain, grad_ffn_bias = layernorm_back(grad_two, hat_two, inv_two, params[2])
    grad_mid = cot_own.astype(F32) + back_two
    x_mid = group_gather(grad_mid.astype(BF16))

    narrow, broad = ((values_all, seq), BF16), ((values_all, width), BF16)
    plain = ((values_all, seq), F32)
    grad_gate, grad_ret, full_go = kernel_call(
        functools.partial(gated_backward, blocks),
        [narrow, narrow, (all_go.shape, BF16)],
        [broad, tall, tall, plain, plain, ((1, seq), F32), narrow, narrow, narrow, broad, broad],
        3 * wide,
        all_go,
        x_one,
        *x_mid,
        gate,
        normed,
        inv_group,
        hidden,
        copies=3 * blocks + 15,
    )
    home_go = home(full_go)
    grad_qkv, full_qkv = kernel_call(
        functools.partial(retention_backward, blocks),
        [((all_qkv.shape[0], seq), BF16), (all_qkv.shape, BF16)],
        [((seq, seq), BF16)],
        2 * seq * width * all_qkv.shape[0] + 2 * square * (keys_all + values_all),
        query,
        keys,
        values,
        weights,
        grad_ret,
        x_one,
        *where,
    )
    home_qkv = home(full_qkv)
    half = home_ud.shape[0] // 2
    grad_up, grad_down = from_wide(home_ud[:half], home_ud[half:])
    (one_part,) = kernel_call(
        functools.partial(input_backward, blocks),
        [((seq, width), BF16)],
        [((values_all, width), BF16)],
        2 * seq * width * all_qkv.shape[0] + wide,
        grad_qkv,
        all_qkv,
        after(grad_gate, full_qkv, grad_up),
        all_go,
    )
    grad_one = group_reduce(one_part)
    (ffn_part,) = kernel_call(
        functools.partial(down_forward, depth),
        [((seq, width), BF16)],
        [((hidden_all, width), BF16)],
        wide_ff,
        all_ud,
        after(act, one_part),
    )
    ffn = group_reduce(ffn_part)
    back_one, grad_attn_gain, grad_attn_bias = layernorm_back(grad_one, hat_one, inv_one, params[0])
    totals = total_over_all(
        jnp.stack([grad_attn_gain, grad_attn_bias, grad_ffn_gain, grad_ffn_bias])
    )
    totals = lax.dynamic_slice_in_dim(totals, lax.axis_index(ROW) * part, part, 1)
    grad_in, block_out = from_wide(
        (grad_mid + back_one).astype(BF16), (middle + ffn).astype(BF16)
    )
    grad_in = grad_in.astype(F32)

    def from_heads(mine):
        send = mine.reshape(2, -1, 4, part).transpose(2, 0, 1, 3).reshape(8, -1, part)
        return lax.all_to_all(send, GROUP, split_axis=0, concat_axis=0, tiled=True)

    def columns(grads, order):
        return dot(grads.reshape(-1, part), order, ((0,), (1,)))

    go = from_heads(ungroup(after(home_go, grad_in), kv, kv))
    back = from_heads(ungroup(after(home_qkv, go, totals), kq, kq, kv))
    grad_up, grad_down = grad_up.T.astype(F32), grad_down.astype(F32)
    out_gate = columns(go[:, :kv], order_v)
    out_out = dot(order_v, go[:, kv:].reshape(-1, part), ((1,), (0,)))
    out_query = columns(back[:, :kq], order_q)
    out_key = columns(back[:, kq : 2 * kq], order_q)
    out_value = columns(back[:, 2 * kq :], order_v)
    return (
        block_out,
        grad_in,
        out_query,
        out_key,
        out_value,
        out_gate,
        out_out,
        grad_up,
        grad_down,
        totals[0],
        totals[1],
        totals[2],
        totals[3],
    )


def solution(mesh):
    rows, cols = mesh.devices.shape
    fine = Mesh(mesh.devices.reshape(rows // 2, 2, cols // 2, 2), ("x", "k", "z", "y"))
    row, col = ("x", "k"), ("z", "y")
    tok, unit = P(col, row), P(row, col)
    return jax.shard_map(
        body,
        mesh=fine,
        in_specs=(tok, tok, P(row), unit, unit, unit, unit, tok, unit, tok)
        + (P(row),) * 4,
        out_specs=(tok, tok, unit, unit, unit, unit, tok, unit, tok) + (P(row),) * 4,
        check_vma=False,
    )
```

```python
import functools
import math

import jax
import jax.numpy as jnp
import numpy as np
from jax import lax
from jax.experimental import pallas as pl
from jax.experimental.pallas import tpu as pltpu
from jax.sharding import Mesh
from jax.sharding import PartitionSpec as P

HEADS = 8
EPS_NORM = 1e-05
EPS_GROUP = 0.25

ROW = ("x", "k")
GROUP = ("x", "k", "y")
EVERY = ("x", "k", "z", "y")
F32 = jnp.float32
BF16 = jnp.bfloat16


def dot(left, right, over):
    return lax.dot_general(left, right, (over, ((), ())), preferred_element_type=F32)


def swap(value, mask):
    return lax.ppermute(value, GROUP, [(i, i ^ mask) for i in range(8)])


def group_gather(part, *others):
    near = [part, swap(part, 1), swap(part, 4), swap(part, 5)]
    far = [swap(after(block, *others), 2) for block in near]
    return near[:2] + far[:2] + near[2:] + far[2:]


def reduce_pairs(total):
    height = total.shape[0] // 8

    def pair(j):
        kept = total[j * height : (j + 1) * height]
        return kept.astype(F32) + swap(total[(j + 2) * height : (j + 3) * height], 2).astype(F32)

    return pair(5).astype(BF16), pair(4), pair(1), pair(0)


def reduce_relay(state):
    across, over_x, over_y, own = state
    half = across.shape[0] // 2
    top, low = swap(across[:half], 1).astype(F32), swap(across[half:], 4).astype(F32)
    over_x = jnp.concatenate([over_x[:half] + top, over_x[half:]], axis=0).astype(BF16)
    over_y = jnp.concatenate([over_y[:half], over_y[half:] + low], axis=0).astype(BF16)
    return over_x, over_y, own


def reduce_last(state):
    over_x, over_y, own = state
    return own + swap(over_x, 4).astype(F32) + swap(over_y, 1).astype(F32)


def group_reduce(total):
    return reduce_last(reduce_relay(reduce_pairs(total)))


def after(value, *others):
    return lax.optimization_barrier((value,) + others)[0]


def total_over_all(value):
    value = value + swap(value, 2)
    value = value + swap(value, 1) + swap(value, 4) + swap(value, 5)
    depth = lax.axis_size("z")
    if depth > 4:
        return lax.psum(value, "z")
    own = value
    for step in range(1, depth):
        value = value + lax.ppermute(own, "z", [(i, (i + step) % depth) for i in range(depth)])
    return value


def row_gather(value):
    got = [value, swap(value, 2), swap(value, 4), swap(value, 6)]
    own = lax.axis_index(ROW)
    rows = []
    for i in range(4):
        picks = [jnp.where((own ^ j) == i, got[j], 0.0) for j in range(4)]
        rows.append(picks[0] + picks[1] + picks[2] + picks[3])
    return jnp.stack(rows)


def row_exchange(parts):
    return lax.all_to_all(parts, ROW, split_axis=0, concat_axis=0, tiled=True)


def to_wide(*parts):
    height, width = parts[0].shape
    moved = row_exchange(jnp.stack([p.reshape(4, -1, width) for p in parts], axis=1))
    moved = moved.transpose(1, 2, 0, 3).reshape(len(parts), height // 4, 4 * width)
    return [moved[i] for i in range(len(parts))]


def from_wide(*parts):
    height, width = parts[0].shape
    moved = row_exchange(
        jnp.stack(parts).reshape(len(parts), height, 4, width // 4).transpose(2, 0, 1, 3)
    )
    moved = moved.transpose(1, 0, 2, 3).reshape(len(parts), 4 * height, width // 4)
    return [moved[i] for i in range(len(parts))]


def head_order(count):
    units = count // HEADS
    j = lax.iota(jnp.int32, count)
    target = (j % HEADS) * units + j // HEADS
    return (target[:, None] == lax.iota(jnp.int32, count)[None, :]).astype(BF16)


def layernorm(value, gain, bias):
    mean = jnp.mean(value, axis=1, keepdims=True)
    centered = value - mean
    inverse = lax.rsqrt(jnp.mean(centered * centered, axis=1, keepdims=True) + EPS_NORM)
    hat = centered * inverse
    return hat, inverse, (hat * gain + bias).astype(BF16)


def layernorm_back(grad, hat, inverse, gain):
    scaled = grad * gain
    first = jnp.mean(scaled, axis=1, keepdims=True)
    second = jnp.mean(scaled * hat, axis=1, keepdims=True)
    return (
        inverse * (scaled - first - hat * second),
        jnp.sum(grad * hat, axis=0),
        jnp.sum(grad, axis=0),
    )


TILE = 256
WIDE = 512
TALL = 512
LIMIT = 58 * 1024 * 1024


def spans(total, tile, step):
    def once(i, carry):
        step(pl.ds(pl.multiple_of(i * tile, tile), tile))
        return carry

    lax.fori_loop(0, total // tile, once, 0)


def kernel_call(body, outs, scratch, flops, *args, copies=0):
    moved = sum(a.size * a.dtype.itemsize for a in args)
    moved += sum(math.prod(shape) * jnp.dtype(kind).itemsize for shape, kind in outs)
    whole = pl.BlockSpec(memory_space=pl.ANY if copies else pltpu.VMEM)
    return pl.pallas_call(
        body,
        out_shape=[jax.ShapeDtypeStruct(shape, kind) for shape, kind in outs],
        in_specs=[whole] * len(args),
        out_specs=[whole] * len(outs),
        scratch_shapes=[pltpu.VMEM(shape, kind) for shape, kind in scratch]
        + [pltpu.SemaphoreType.DMA((copies,))] * bool(copies),
        compiler_params=pltpu.CompilerParams(vmem_limit_bytes=LIMIT),
        cost_estimate=pl.CostEstimate(flops=flops, bytes_accessed=moved, transcendentals=0),
    )(*args)


def unpack(source, first, second, depth):
    half = source.shape[0] // (2 * depth)
    for i in range(depth):
        at = 2 * i * half
        if first is not None:
            first[i * half : (i + 1) * half, :] = source[at : at + half, :]
        if second is not None:
            second[i * half : (i + 1) * half, :] = source[at + half : at + 2 * half, :]


def pack(target, columns, first, second, depth):
    half = first.shape[0] // depth
    for i in range(depth):
        at = 2 * i * half
        target[at : at + half, columns] = first[i * half : (i + 1) * half]
        target[at + half : at + 2 * half, columns] = second[i * half : (i + 1) * half]


def decayed(raw, spot, segs, grow, fall, rows):
    inside = (spot[0][rows, :] >= spot[1][...]) & (segs[0][rows, :] == segs[1][...])
    return jnp.where(inside, raw * (grow[rows, :] * fall[...]), 0.0).astype(BF16)


def retention_forward(depth, w, x, pc, pr, sc, sr, grow, fall, q, k, v, weights, normed, inv):
    seq = x.shape[0]
    part = q.shape[0] // depth
    width = v.shape[0] // depth
    group = 2 * part + width

    def project(at):
        out = dot(w[...], x[at, :], ((1,), (1,))).astype(BF16)
        for i in range(depth):
            z = i * group
            q[i * part : (i + 1) * part, at] = out[z : z + part]
            k[i * part : (i + 1) * part, at] = out[z + part : z + 2 * part]
            v[i * width : (i + 1) * width, at] = out[z + 2 * part : z + group]

    def attend(at):
        raw = dot(q[:, at], k[...], ((0,), (0,)))
        low = decayed(raw, (pc, pr), (sc, sr), grow, fall, at)
        weights[at, :] = low
        kept = dot(v[...], low, ((1,), (1,)))
        centered = kept - jnp.mean(kept, axis=0, keepdims=True)
        scale = lax.rsqrt(jnp.mean(centered * centered, axis=0, keepdims=True) + EPS_GROUP)
        normed[:, at] = centered * scale
        inv[:, at] = scale

    spans(seq, TILE, project)
    spans(seq, TILE, attend)


def gated_forward(depth, w, x, normed, gate, hidden, out, wg, wo):
    unpack(w, wg, wo, depth)

    def step(at):
        g = dot(wg[...], x[at, :], ((1,), (1,)))
        gate[:, at] = g
        low = normed[:, at].astype(BF16).astype(F32)
        h = (g * jax.nn.sigmoid(g) * low).astype(BF16)
        hidden[:, at] = h
        out[at, :] = dot(h, wo[...], ((0,), (0,))).astype(BF16)

    spans(x.shape[0], TILE, step)


class Mover:
    def __init__(self, semaphores):
        self.semaphores = semaphores
        self.count = 0

    def start(self, source, target):
        copy = pltpu.make_async_copy(source, target, self.semaphores.at[self.count])
        self.count += 1
        copy.start()
        return copy

    def rows(self, sources, target):
        height = sources[0].shape[0]
        return [
            self.start(source, target.at[pl.ds(i * height, height)])
            for i, source in enumerate(sources)
        ]

    def kind(self, source, target, which, depth):
        half = (source if which[0] == "from" else target).shape[0] // (2 * depth)
        moved = []
        for i in range(depth):
            mixed = pl.ds((2 * i + which[1]) * half, half)
            plain = pl.ds(i * half, half)
            if which[0] == "from":
                moved.append(self.start(source.at[mixed], target.at[plain]))
            else:
                moved.append(self.start(source.at[plain], target.at[mixed]))
        return moved


def wait(copies):
    for copy in copies:
        copy.wait()


def feedforward(depth, w, *refs):
    x_blocks, cot_blocks = refs[:8], refs[8:16]
    act_out, back_out, grads_out = refs[16:19]
    wu, wd, x, cot, act, gp, turned, back, gu, gd, semaphores = refs[19:]
    move = Mover(semaphores)
    seq, rows = x.shape[0], x_blocks[0].shape[0]
    weights = move.kind(w, wu, ("from", 0), depth) + move.kind(w, wd, ("from", 1), depth)
    x_copies, cot_copies = move.rows(x_blocks, x), move.rows(cot_blocks, cot)
    wait(weights)
    for tile in range(seq // TALL):
        mine = slice(tile * TALL // rows, (tile + 1) * TALL // rows)
        wait(x_copies[mine] + cot_copies[mine])
        at = pl.ds(tile * TALL, TALL)
        pre = dot(wu[...], x[at, :], ((1,), (1,)))
        grad = dot(wd[...], cot[at, :], ((1,), (1,)))
        half = 0.5 * (1.0 + lax.erf(pre * np.float32(0.5**0.5)))
        act[:, at] = (pre * half).astype(BF16)
        bell = jnp.exp(-0.5 * pre * pre) * np.float32((2 * math.pi) ** -0.5)
        low = grad * (half + pre * bell)
        gp[:, at] = low.astype(BF16)
        turned[at, :] = low.T.astype(BF16)
    sent = [move.start(act, act_out)]

    def up_step(at):
        gu[:, at] = dot(gp[...], x[:, at], ((1,), (0,))).astype(BF16)

    def down_step(at):
        gd[:, at] = dot(act[...], cot[:, at], ((1,), (0,))).astype(BF16)

    spans(x.shape[1], WIDE, up_step)
    sent += move.kind(gu, grads_out, ("to", 0), depth)
    spans(x.shape[1], WIDE, down_step)
    sent += move.kind(gd, grads_out, ("to", 1), depth)
    for tile in range(x.shape[1] // WIDE):
        at = pl.ds(tile * WIDE, WIDE)
        back[:, at] = dot(turned[...], wu[:, at], ((1,), (0,))).astype(BF16)
        sent.append(move.start(back.at[:, at], back_out.at[:, at]))
    wait(sent)


def down_forward(depth, w, act, out, wd):
    unpack(w, None, wd, depth)

    def step(at):
        out[at, :] = dot(act[:, at], wd[...], ((0,), (0,))).astype(BF16)

    spans(act.shape[1], TILE, step)


def gated_backward(depth, w, x_in, *refs):
    mid_blocks = refs[:8]
    gate_in, normed_in, inv_in, hidden_in, ggate_out, gret_out, grads_out = refs[8:15]
    wo, x, mid, gate, normed, inv, hidden, ggate, gret, gg, go, semaphores = refs[15:]
    move = Mover(semaphores)
    seq, rows = x.shape[0], mid_blocks[0].shape[0]
    first = move.kind(w, wo, ("from", 1), depth)
    mid_copies = move.rows(mid_blocks[:4], mid.at[pl.ds(0, 4 * rows)])
    first += [move.start(inv_in, inv), move.start(gate_in, gate), move.start(normed_in, normed)]
    mid_copies += move.rows(mid_blocks[4:], mid.at[pl.ds(4 * rows, seq - 4 * rows)])
    late = [move.start(x_in, x), move.start(hidden_in, hidden)]
    wait(first)
    for tile in range(seq // TALL):
        wait(mid_copies[tile * TALL // rows : (tile + 1) * TALL // rows])
        at = pl.ds(tile * TALL, TALL)
        up = dot(wo[...], mid[at, :], ((1,), (1,)))
        g = gate[:, at]
        s = jax.nn.sigmoid(g)
        full = normed[:, at]
        low = full.astype(BF16).astype(F32)
        ggate[:, at] = (up * low * (s * (1.0 + g * (1.0 - s)))).astype(BF16)
        gn = (up * (g * s)).astype(BF16).astype(F32)
        mean = jnp.mean(gn, axis=0, keepdims=True)
        slope = jnp.mean(gn * full, axis=0, keepdims=True)
        gret[:, at] = (inv[:, at] * (gn - mean - full * slope)).astype(BF16)
    sent = [move.start(ggate, ggate_out), move.start(gret, gret_out)]
    wait(late)

    def gate_step(at):
        gg[:, at] = dot(ggate[...], x[:, at], ((1,), (0,))).astype(BF16)

    def out_step(at):
        go[:, at] = dot(hidden[...], mid[:, at], ((1,), (0,))).astype(BF16)

    spans(x.shape[1], WIDE, gate_step)
    sent += move.kind(gg, grads_out, ("to", 0), depth)
    spans(x.shape[1], WIDE, out_step)
    sent += move.kind(go, grads_out, ("to", 1), depth)
    wait(sent)


def retention_backward(
    depth, q, k, v, weights, gret, x, pc, pr, sc, sr, grow, fall, packed, grads, scores
):
    seq = x.shape[0]
    part = q.shape[0] // depth
    width = v.shape[0] // depth
    group = 2 * part + width

    def place(value, at, offset, height):
        for i in range(depth):
            z = i * group + offset
            packed[z : z + height, at] = value[i * height : (i + 1) * height]

    def query_step(at):
        raw = dot(gret[:, at], v[...], ((0,), (0,)))
        low = decayed(raw, (pc, pr), (sc, sr), grow, fall, at)
        scores[at, :] = low
        place(dot(k[...], low, ((1,), (1,))).astype(BF16), at, 0, part)

    def key_step(at):
        place(dot(q[...], scores[:, at], ((1,), (0,))).astype(BF16), at, part, part)
        place(dot(gret[...], weights[:, at], ((1,), (0,))).astype(BF16), at, 2 * part, width)

    spans(seq, TILE, query_step)
    spans(seq, TILE, key_step)
    if len(grads.shape) == 2:

        def grad_step(at):
            grads[:, at] = dot(packed[...], x[:, at], ((1,), (0,))).astype(BF16)

        spans(x.shape[1], WIDE, grad_step)
        return

    def home_step(row, carry):
        columns = grads.shape[3]
        at = pl.ds(pl.multiple_of(row * columns, columns), columns)
        full = dot(packed[...], x[:, at], ((1,), (0,))).astype(BF16)
        for i in range(depth):
            grads[i // 2, 2 * row + i % 2, :, :] = full[i * group : (i + 1) * group]
        return carry

    lax.fori_loop(0, 4, home_step, 0)


def input_backward(depth, packed, w, ggate, wgo, out, wg):
    unpack(wgo, wg, None, depth)

    def step(at):
        total = dot(packed[:, at], w[...], ((0,), (0,)))
        out[at, :] = (total + dot(ggate[:, at], wg[...], ((0,), (0,)))).astype(BF16)

    spans(packed.shape[1], TILE, step)


def body(
    block_in,
    cotangent,
    segments,
    w_query,
    w_key,
    w_value,
    w_gate,
    w_out,
    w_up,
    w_down,
    retention_norm_gain,
    retention_norm_bias,
    feedforward_norm_gain,
    feedforward_norm_bias,
):
    depth = lax.axis_size("z")
    part = block_in.shape[1]
    width = 4 * part
    own = lax.axis_index(GROUP)
    plane = lax.axis_index("z")
    tokens = block_in.shape[0] // 4
    seq = 8 * tokens

    kq = w_query.shape[1] // HEADS
    kv = w_value.shape[1] // HEADS
    order_q = head_order(w_query.shape[1])
    order_v = head_order(w_value.shape[1])

    def by_head(weight, order):
        return dot(order, weight, ((0,), (1,))).astype(BF16).reshape(HEADS, -1, part)

    def to_heads(send):
        got = lax.all_to_all(send, GROUP, split_axis=0, concat_axis=0, tiled=True)
        got = got.reshape(4, 2, send.shape[1], part).transpose(1, 2, 0, 3)
        return got.reshape(2, send.shape[1], width)

    split = 2 if kq % 16 == 0 else 1
    blocks = depth * split

    def regroup(rows, *counts):
        if split == 2:
            return rows.reshape(-1, width)
        cuts = np.cumsum((0,) + counts)
        return jnp.concatenate(
            [rows[:, cuts[i] : cuts[i + 1]].reshape(-1, width) for i in range(len(counts))]
        )

    def ungroup(rows, *counts):
        if split == 2:
            return rows.reshape(2, -1, width)
        cuts = 2 * np.cumsum((0,) + counts)
        return jnp.concatenate(
            [rows[cuts[i] : cuts[i + 1]].reshape(2, -1, width) for i in range(len(counts))], axis=1
        )

    def planes(mine):
        return lax.all_gather(mine, "z", axis=0, tiled=True)

    got_qkv = to_heads(
        jnp.concatenate(
            [by_head(w_query, order_q), by_head(w_key, order_q), by_head(w_value, order_v)], axis=1
        )
    )
    mine_qkv = regroup(got_qkv, kq, kq, kv)
    all_qkv = planes(mine_qkv)
    send_go = jnp.concatenate(
        [
            by_head(w_gate, order_v),
            dot(order_v, w_out, ((0,), (0,))).astype(BF16).reshape(HEADS, -1, part),
        ],
        axis=1,
    )
    got_go = to_heads(after(send_go, mine_qkv))
    mine_go = regroup(got_go, kv, kv)
    all_go = planes(mine_go)

    small = jnp.concatenate(
        [
            retention_norm_gain,
            retention_norm_bias,
            feedforward_norm_gain,
            feedforward_norm_bias,
            segments.astype(F32),
        ]
    )
    small = row_gather(after(small, mine_qkv))
    params = small[:, : 4 * part].reshape(4, 4, part).transpose(1, 0, 2).reshape(4, width)
    segs = small[:, 4 * part :].astype(jnp.int32).reshape(depth, 8, tokens)
    block_in, cotangent = after(block_in, got_go), after(cotangent, got_go)
    stream_low, cot_own = to_wide(block_in, cotangent)
    mine_up, mine_down = to_wide(after(w_up, stream_low).T, after(w_down, stream_low))
    all_ud = planes(after(jnp.concatenate([mine_up, mine_down], axis=0), mine_go))
    stream = stream_low.astype(F32)
    hat_one, inv_one, norm_one = layernorm(stream, params[0], params[1])
    x_one = jnp.concatenate(group_gather(norm_one), axis=0)

    ids = lax.iota(jnp.int32, 8) ^ own
    ids = (ids % 2) * 4 + ids // 2
    picked = (ids[:, None] == lax.iota(jnp.int32, 8)[None, :])[:, :, None]
    here = (lax.iota(jnp.int32, depth) == plane)[:, None, None]
    seg_plane = jnp.sum(jnp.where(here, segs, 0), axis=0)
    seg = jnp.sum(jnp.where(picked, seg_plane[None], 0), axis=1).reshape(seq)
    pos = (ids[:, None] * tokens + lax.iota(jnp.int32, tokens)[None, :]).reshape(seq)

    loggam = jnp.log1p(-jnp.exp2(-5.0 - own.astype(F32)))
    lag = (pos - seq // 2).astype(F32) * loggam
    grow = jnp.exp(lag) * np.float32((kq * 2 * depth) ** (-0.5))
    where = (pos[:, None], pos[None, :], seg[:, None], seg[None, :])
    where = where + (grow[:, None], jnp.exp(-lag)[None, :])

    x_one = after(x_one, mine_up, mine_down)
    keys_all, values_all = kq * 2 * depth, kv * 2 * depth
    square = 2 * seq * seq
    query, keys, values, weights, normed, inv_group = kernel_call(
        functools.partial(retention_forward, blocks),
        [
            ((keys_all, seq), BF16),
            ((keys_all, seq), BF16),
            ((values_all, seq), BF16),
            ((seq, seq), BF16),
            ((values_all, seq), F32),
            ((1, seq), F32),
        ],
        [],
        2 * seq * width * all_qkv.shape[0] + square * (keys_all + values_all),
        all_qkv,
        x_one,
        *where,
    )
    cot = group_gather(after(cot_own, x_one))
    wide = 2 * seq * width * values_all
    gate, hidden, attn = kernel_call(
        functools.partial(gated_forward, blocks),
        [((values_all, seq), F32), ((values_all, seq), BF16), ((seq, width), BF16)],
        [((values_all, width), BF16), ((values_all, width), BF16)],
        2 * wide,
        all_go,
        x_one,
        after(normed, cot),
    )
    middle = stream + group_reduce(attn)

    hat_two, inv_two, norm_two = layernorm(middle, params[2], params[3])
    x_two = group_gather(norm_two)
    token = swap(after(norm_two[:8, :128], all_ud), 2)
    hidden_all = all_ud.shape[0] // 2
    wide_ff = 2 * seq * width * hidden_all
    narrow, broad = ((hidden_all, seq), BF16), ((hidden_all, width), BF16)
    tall = ((seq, width), BF16)
    act, two_part, full_ud = kernel_call(
        functools.partial(feedforward, depth),
        [narrow, tall, (all_ud.shape, BF16)],
        [broad, broad, tall, tall, narrow, narrow, ((seq, hidden_all), BF16), tall, broad, broad],
        5 * wide_ff,
        all_ud,
        *x_two,
        after(cot[0], token),
        *cot[1:],
        copies=4 * depth + 17 + width // WIDE,
    )
    grad_two = group_reduce(two_part)

    def home(full):
        return lax.psum_scatter(full, "z", scatter_dimension=0, tiled=True)

    def from_units(mine):
        send = mine.reshape(-1, 4, part).transpose(1, 0, 2)
        return row_exchange(send).reshape(-1, part)

    home_ud = home(full_ud)

    back_two, grad_ffn_gain, grad_ffn_bias = layernorm_back(grad_two, hat_two, inv_two, params[2])
    grad_mid = cot_own.astype(F32) + back_two
    x_mid = group_gather(grad_mid.astype(BF16))

    narrow, broad = ((values_all, seq), BF16), ((values_all, width), BF16)
    plain = ((values_all, seq), F32)
    grad_gate, grad_ret, full_go = kernel_call(
        functools.partial(gated_backward, blocks),
        [narrow, narrow, (all_go.shape, BF16)],
        [broad, tall, tall, plain, plain, ((1, seq), F32), narrow, narrow, narrow, broad, broad],
        3 * wide,
        all_go,
        x_one,
        *x_mid,
        gate,
        normed,
        inv_group,
        hidden,
        copies=3 * blocks + 15,
    )
    home_go = home(full_go)
    home_shape = (depth, 8, 2 * kq + kv, part) if split == 2 else all_qkv.shape
    grad_qkv, full_qkv = kernel_call(
        functools.partial(retention_backward, blocks),
        [((all_qkv.shape[0], seq), BF16), (home_shape, BF16)],
        [((seq, seq), BF16)],
        2 * seq * width * all_qkv.shape[0] + 2 * square * (keys_all + values_all),
        query,
        keys,
        values,
        weights,
        grad_ret,
        x_one,
        *where,
    )
    home_qkv = home(full_qkv)
    half = home_ud.shape[0] // 2
    grad_up, grad_down = from_wide(home_ud[:half], home_ud[half:])
    (one_part,) = kernel_call(
        functools.partial(input_backward, blocks),
        [((seq, width), BF16)],
        [((values_all, width), BF16)],
        2 * seq * width * all_qkv.shape[0] + wide,
        grad_qkv,
        all_qkv,
        after(grad_gate, full_qkv, grad_up),
        all_go,
    )
    grad_one = group_reduce(one_part)
    (ffn_part,) = kernel_call(
        functools.partial(down_forward, depth),
        [((seq, width), BF16)],
        [((hidden_all, width), BF16)],
        wide_ff,
        all_ud,
        after(act, one_part),
    )
    ffn = group_reduce(ffn_part)
    back_one, grad_attn_gain, grad_attn_bias = layernorm_back(grad_one, hat_one, inv_one, params[0])
    totals = total_over_all(
        jnp.stack([grad_attn_gain, grad_attn_bias, grad_ffn_gain, grad_ffn_bias])
    )
    totals = lax.dynamic_slice_in_dim(totals, lax.axis_index(ROW) * part, part, 1)
    grad_in, block_out = from_wide(
        (grad_mid + back_one).astype(BF16), (middle + ffn).astype(BF16)
    )
    grad_in = grad_in.astype(F32)

    def from_heads(mine):
        send = mine.reshape(2, -1, 4, part).transpose(2, 0, 1, 3).reshape(8, -1, part)
        return lax.all_to_all(send, GROUP, split_axis=0, concat_axis=0, tiled=True)

    def columns(grads, order):
        return dot(grads.reshape(-1, part), order, ((0,), (1,)))

    go = from_heads(ungroup(after(home_go, grad_in), kv, kv))
    home_qkv = after(home_qkv, go, totals)
    if split == 2:
        home_qkv = home_qkv.reshape(8, 2 * kq + kv, part)
        back = lax.all_to_all(home_qkv, GROUP, split_axis=0, concat_axis=0, tiled=True)
    else:
        back = from_heads(ungroup(home_qkv, kq, kq, kv))
    grad_up, grad_down = grad_up.T.astype(F32), grad_down.astype(F32)
    out_gate = columns(go[:, :kv], order_v)
    out_out = dot(order_v, go[:, kv:].reshape(-1, part), ((1,), (0,)))
    out_query = columns(back[:, :kq], order_q)
    out_key = columns(back[:, kq : 2 * kq], order_q)
    out_value = columns(back[:, 2 * kq :], order_v)
    return (
        block_out,
        grad_in,
        out_query,
        out_key,
        out_value,
        out_gate,
        out_out,
        grad_up,
        grad_down,
        totals[0],
        totals[1],
        totals[2],
        totals[3],
    )


def solution(mesh):
    rows, cols = mesh.devices.shape
    fine = Mesh(mesh.devices.reshape(rows // 2, 2, cols // 2, 2), ("x", "k", "z", "y"))
    row, col = ("x", "k"), ("z", "y")
    tok, unit = P(col, row), P(row, col)
    return jax.shard_map(
        body,
        mesh=fine,
        in_specs=(tok, tok, P(row), unit, unit, unit, unit, tok, unit, tok)
        + (P(row),) * 4,
        out_specs=(tok, tok, unit, unit, unit, unit, tok, unit, tok) + (P(row),) * 4,
        check_vma=False,
    )
```

```python
import functools
import math

import jax
import jax.numpy as jnp
import numpy as np
from jax import lax
from jax.experimental import pallas as pl
from jax.experimental.pallas import tpu as pltpu
from jax.sharding import Mesh
from jax.sharding import PartitionSpec as P

HEADS = 8
EPS_NORM = 1e-05
EPS_GROUP = 0.25

ROW = ("x", "k")
GROUP = ("x", "k", "y")
EVERY = ("x", "k", "z", "y")
F32 = jnp.float32
BF16 = jnp.bfloat16


def dot(left, right, over):
    return lax.dot_general(left, right, (over, ((), ())), preferred_element_type=F32)


def swap(value, mask):
    return lax.ppermute(value, GROUP, [(i, i ^ mask) for i in range(8)])


def group_gather(part, *others):
    near = [part, swap(part, 1), swap(part, 4), swap(part, 5)]
    far = [swap(after(block, *others), 2) for block in near]
    return near[:2] + far[:2] + near[2:] + far[2:]


def reduce_pairs(total):
    height = total.shape[0] // 8

    def pair(j):
        kept = total[j * height : (j + 1) * height]
        return kept.astype(F32) + swap(total[(j + 2) * height : (j + 3) * height], 2).astype(F32)

    return pair(5).astype(BF16), pair(4), pair(1), pair(0)


def reduce_relay(state):
    across, over_x, over_y, own = state
    half = across.shape[0] // 2
    top, low = swap(across[:half], 1).astype(F32), swap(across[half:], 4).astype(F32)
    over_x = jnp.concatenate([over_x[:half] + top, over_x[half:]], axis=0).astype(BF16)
    over_y = jnp.concatenate([over_y[:half], over_y[half:] + low], axis=0).astype(BF16)
    return over_x, over_y, own


def reduce_last(state):
    over_x, over_y, own = state
    return own + swap(over_x, 4).astype(F32) + swap(over_y, 1).astype(F32)


def group_reduce(total):
    return reduce_last(reduce_relay(reduce_pairs(total)))


def after(value, *others):
    return lax.optimization_barrier((value,) + others)[0]


def total_over_all(value):
    value = value + swap(value, 2)
    value = value + swap(value, 1) + swap(value, 4) + swap(value, 5)
    depth = lax.axis_size("z")
    if depth > 4:
        return lax.psum(value, "z")
    own = value
    for step in range(1, depth):
        value = value + lax.ppermute(own, "z", [(i, (i + step) % depth) for i in range(depth)])
    return value


def row_gather(value):
    got = [value, swap(value, 2), swap(value, 4), swap(value, 6)]
    own = lax.axis_index(ROW)
    rows = []
    for i in range(4):
        picks = [jnp.where((own ^ j) == i, got[j], 0.0) for j in range(4)]
        rows.append(picks[0] + picks[1] + picks[2] + picks[3])
    return jnp.stack(rows)


def row_exchange(parts):
    return lax.all_to_all(parts, ROW, split_axis=0, concat_axis=0, tiled=True)


def to_wide(*parts):
    height, width = parts[0].shape
    moved = row_exchange(jnp.stack([p.reshape(4, -1, width) for p in parts], axis=1))
    moved = moved.transpose(1, 2, 0, 3).reshape(len(parts), height // 4, 4 * width)
    return [moved[i] for i in range(len(parts))]


def from_wide(*parts):
    height, width = parts[0].shape
    moved = row_exchange(
        jnp.stack(parts).reshape(len(parts), height, 4, width // 4).transpose(2, 0, 1, 3)
    )
    moved = moved.transpose(1, 0, 2, 3).reshape(len(parts), 4 * height, width // 4)
    return [moved[i] for i in range(len(parts))]


def head_order(count):
    units = count // HEADS
    j = lax.iota(jnp.int32, count)
    target = (j % HEADS) * units + j // HEADS
    return (target[:, None] == lax.iota(jnp.int32, count)[None, :]).astype(BF16)


def layernorm(value, gain, bias):
    mean = jnp.mean(value, axis=1, keepdims=True)
    centered = value - mean
    inverse = lax.rsqrt(jnp.mean(centered * centered, axis=1, keepdims=True) + EPS_NORM)
    hat = centered * inverse
    return hat, inverse, (hat * gain + bias).astype(BF16)


def layernorm_back(grad, hat, inverse, gain):
    scaled = grad * gain
    first = jnp.mean(scaled, axis=1, keepdims=True)
    second = jnp.mean(scaled * hat, axis=1, keepdims=True)
    return (
        inverse * (scaled - first - hat * second),
        jnp.sum(grad * hat, axis=0),
        jnp.sum(grad, axis=0),
    )


TILE = 256
WIDE = 512
TALL = 512
LIMIT = 58 * 1024 * 1024


def spans(total, tile, step):
    def once(i, carry):
        step(pl.ds(pl.multiple_of(i * tile, tile), tile))
        return carry

    lax.fori_loop(0, total // tile, once, 0)


def kernel_call(body, outs, scratch, flops, *args, copies=0):
    moved = sum(a.size * a.dtype.itemsize for a in args)
    moved += sum(math.prod(shape) * jnp.dtype(kind).itemsize for shape, kind in outs)
    whole = pl.BlockSpec(memory_space=pl.ANY if copies else pltpu.VMEM)
    return pl.pallas_call(
        body,
        out_shape=[jax.ShapeDtypeStruct(shape, kind) for shape, kind in outs],
        in_specs=[whole] * len(args),
        out_specs=[whole] * len(outs),
        scratch_shapes=[pltpu.VMEM(shape, kind) for shape, kind in scratch]
        + [pltpu.SemaphoreType.DMA((copies,))] * bool(copies),
        compiler_params=pltpu.CompilerParams(vmem_limit_bytes=LIMIT),
        cost_estimate=pl.CostEstimate(flops=flops, bytes_accessed=moved, transcendentals=0),
    )(*args)


def unpack(source, targets, depth):
    height = source.shape[0] // (len(targets) * depth)
    for i in range(depth):
        for j, target in enumerate(targets):
            at = (i * len(targets) + j) * height
            if target is not None:
                target[i * height : (i + 1) * height, :] = source[at : at + height, :]


def decayed(raw, spot, segs, grow, fall, rows):
    inside = (spot[0][rows, :] >= spot[1][...]) & (segs[0][rows, :] == segs[1][...])
    return jnp.where(inside, raw * (grow[rows, :] * fall[...]), 0.0).astype(BF16)


def retention_scores(depth, w, x, pc, pr, sc, sr, grow, fall, q, k, weights):
    seq = x.shape[0]
    part = q.shape[0] // depth

    def project(at):
        out = dot(w[...], x[at, :], ((1,), (1,))).astype(BF16)
        for i in range(depth):
            z = 2 * i * part
            q[i * part : (i + 1) * part, at] = out[z : z + part]
            k[i * part : (i + 1) * part, at] = out[z + part : z + 2 * part]

    def attend(at):
        raw = dot(q[:, at], k[...], ((0,), (0,)))
        weights[at, :] = decayed(raw, (pc, pr), (sc, sr), grow, fall, at)

    spans(seq, TILE, project)
    spans(seq, TILE, attend)


def gated_forward(depth, w, x, weights, gate, hidden, out, v, normed, inv, wv, wg, wo):
    unpack(w, (wv, wg, wo), depth)

    def project(at):
        v[:, at] = dot(wv[...], x[at, :], ((1,), (1,))).astype(BF16)

    def step(at):
        kept = dot(v[...], weights[at, :], ((1,), (1,)))
        centered = kept - jnp.mean(kept, axis=0, keepdims=True)
        scale = lax.rsqrt(jnp.mean(centered * centered, axis=0, keepdims=True) + EPS_GROUP)
        full = centered * scale
        normed[:, at] = full
        inv[:, at] = scale
        g = dot(wg[...], x[at, :], ((1,), (1,)))
        gate[:, at] = g
        h = (g * jax.nn.sigmoid(g) * full.astype(BF16).astype(F32)).astype(BF16)
        hidden[:, at] = h
        out[at, :] = dot(h, wo[...], ((0,), (0,))).astype(BF16)

    spans(x.shape[0], TILE, project)
    spans(x.shape[0], TILE, step)


class Mover:
    def __init__(self, semaphores):
        self.semaphores = semaphores
        self.count = 0

    def start(self, source, target):
        copy = pltpu.make_async_copy(source, target, self.semaphores.at[self.count])
        self.count += 1
        copy.start()
        return copy

    def rows(self, sources, target):
        height = sources[0].shape[0]
        return [
            self.start(source, target.at[pl.ds(i * height, height)])
            for i, source in enumerate(sources)
        ]

    def kind(self, source, target, which, depth):
        way, index, kinds = which
        height = (source if way == "from" else target).shape[0] // (kinds * depth)
        moved = []
        for i in range(depth):
            mixed = pl.ds((kinds * i + index) * height, height)
            plain = pl.ds(i * height, height)
            if way == "from":
                moved.append(self.start(source.at[mixed], target.at[plain]))
            else:
                moved.append(self.start(source.at[plain], target.at[mixed]))
        return moved


def wait(copies):
    for copy in copies:
        copy.wait()


def feedforward(depth, w, *refs):
    x_blocks, cot_blocks = refs[:8], refs[8:16]
    act_out, back_out, grads_out = refs[16:19]
    wu, wd, x, cot, act, gp, turned, back, gu, gd, semaphores = refs[19:]
    move = Mover(semaphores)
    seq, rows = x.shape[0], x_blocks[0].shape[0]
    weights = move.kind(w, wu, ("from", 0, 2), depth) + move.kind(w, wd, ("from", 1, 2), depth)
    x_copies, cot_copies = move.rows(x_blocks, x), move.rows(cot_blocks, cot)
    wait(weights)
    for tile in range(seq // TALL):
        mine = slice(tile * TALL // rows, (tile + 1) * TALL // rows)
        wait(x_copies[mine] + cot_copies[mine])
        at = pl.ds(tile * TALL, TALL)
        pre = dot(wu[...], x[at, :], ((1,), (1,)))
        grad = dot(wd[...], cot[at, :], ((1,), (1,)))
        half = 0.5 * (1.0 + lax.erf(pre * np.float32(0.5**0.5)))
        act[:, at] = (pre * half).astype(BF16)
        bell = jnp.exp(-0.5 * pre * pre) * np.float32((2 * math.pi) ** -0.5)
        low = grad * (half + pre * bell)
        gp[:, at] = low.astype(BF16)
        turned[at, :] = low.T.astype(BF16)
    sent = [move.start(act, act_out)]

    def up_step(at):
        gu[:, at] = dot(gp[...], x[:, at], ((1,), (0,))).astype(BF16)

    def down_step(at):
        gd[:, at] = dot(act[...], cot[:, at], ((1,), (0,))).astype(BF16)

    spans(x.shape[1], WIDE, up_step)
    sent += move.kind(gu, grads_out, ("to", 0, 2), depth)
    spans(x.shape[1], WIDE, down_step)
    sent += move.kind(gd, grads_out, ("to", 1, 2), depth)
    for tile in range(x.shape[1] // WIDE):
        at = pl.ds(tile * WIDE, WIDE)
        back[:, at] = dot(turned[...], wu[:, at], ((1,), (0,))).astype(BF16)
        sent.append(move.start(back.at[:, at], back_out.at[:, at]))
    wait(sent)


def down_forward(depth, w, act, out, wd):
    unpack(w, (None, wd), depth)

    def step(at):
        out[at, :] = dot(act[:, at], wd[...], ((0,), (0,))).astype(BF16)

    spans(act.shape[1], TILE, step)


def gated_backward(depth, w, x_in, *refs):
    mid_blocks = refs[:8]
    gate_in, normed_in, inv_in, hidden_in, ggate_out, gret_out, grads_out = refs[8:15]
    wo, x, mid, gate, normed, inv, hidden, ggate, gret, gg, go, semaphores = refs[15:]
    move = Mover(semaphores)
    seq, rows = x.shape[0], mid_blocks[0].shape[0]
    first = move.kind(w, wo, ("from", 2, 3), depth)
    mid_copies = move.rows(mid_blocks[:4], mid.at[pl.ds(0, 4 * rows)])
    first += [move.start(inv_in, inv), move.start(gate_in, gate), move.start(normed_in, normed)]
    mid_copies += move.rows(mid_blocks[4:], mid.at[pl.ds(4 * rows, seq - 4 * rows)])
    late = [move.start(x_in, x), move.start(hidden_in, hidden)]
    wait(first)
    for tile in range(seq // TALL):
        wait(mid_copies[tile * TALL // rows : (tile + 1) * TALL // rows])
        at = pl.ds(tile * TALL, TALL)
        up = dot(wo[...], mid[at, :], ((1,), (1,)))
        g = gate[:, at]
        s = jax.nn.sigmoid(g)
        full = normed[:, at]
        low = full.astype(BF16).astype(F32)
        ggate[:, at] = (up * low * (s * (1.0 + g * (1.0 - s)))).astype(BF16)
        gn = (up * (g * s)).astype(BF16).astype(F32)
        mean = jnp.mean(gn, axis=0, keepdims=True)
        slope = jnp.mean(gn * full, axis=0, keepdims=True)
        gret[:, at] = (inv[:, at] * (gn - mean - full * slope)).astype(BF16)
    sent = [move.start(ggate, ggate_out), move.start(gret, gret_out)]
    wait(late)

    def gate_step(at):
        gg[:, at] = dot(ggate[...], x[:, at], ((1,), (0,))).astype(BF16)

    def out_step(at):
        go[:, at] = dot(hidden[...], mid[:, at], ((1,), (0,))).astype(BF16)

    spans(x.shape[1], WIDE, gate_step)
    sent += move.kind(gg, grads_out, ("to", 0, 2), depth)
    spans(x.shape[1], WIDE, out_step)
    sent += move.kind(go, grads_out, ("to", 1, 2), depth)
    wait(sent)


def retention_backward(
    depth, q, k, v, weights, gret, x, pc, pr, sc, sr, grow, fall, packed, grads, scores
):
    seq = x.shape[0]
    part = q.shape[0] // depth
    width = v.shape[0] // depth
    pairs = 2 * part * depth

    def place(value, at, offset):
        for i in range(depth):
            z = 2 * i * part + offset
            packed[z : z + part, at] = value[i * part : (i + 1) * part]

    def query_step(at):
        raw = dot(gret[:, at], v[...], ((0,), (0,)))
        low = decayed(raw, (pc, pr), (sc, sr), grow, fall, at)
        scores[at, :] = low
        place(dot(k[...], low, ((1,), (1,))).astype(BF16), at, 0)

    def key_step(at):
        place(dot(q[...], scores[:, at], ((1,), (0,))).astype(BF16), at, part)
        packed[pairs:, at] = dot(gret[...], weights[:, at], ((1,), (0,))).astype(BF16)

    spans(seq, TILE, query_step)
    spans(seq, TILE, key_step)
    if len(grads.shape) == 2:

        def grad_step(at):
            full = dot(packed[...], x[:, at], ((1,), (0,))).astype(BF16)
            for i in range(depth):
                z = i * (2 * part + width)
                grads[z : z + 2 * part, at] = full[2 * i * part : 2 * (i + 1) * part]
                grads[z + 2 * part : z + 2 * part + width, at] = full[
                    pairs + i * width : pairs + (i + 1) * width
                ]

        spans(x.shape[1], WIDE, grad_step)
        return

    def home_step(row, carry):
        columns = grads.shape[3]
        at = pl.ds(pl.multiple_of(row * columns, columns), columns)
        full = dot(packed[...], x[:, at], ((1,), (0,))).astype(BF16)
        for i in range(depth):
            there = (i // 2, 2 * row + i % 2)
            grads[(*there, slice(0, 2 * part))] = full[2 * i * part : 2 * (i + 1) * part]
            grads[(*there, slice(2 * part, 2 * part + width))] = full[
                pairs + i * width : pairs + (i + 1) * width
            ]
        return carry

    lax.fori_loop(0, 4, home_step, 0)


def input_backward(depth, packed, w, ggate, vgo, out, wv, wg):
    unpack(vgo, (wv, wg, None), depth)
    pairs = w.shape[0]

    def step(at):
        total = dot(packed[:pairs, at], w[...], ((0,), (0,)))
        total = total + dot(packed[pairs:, at], wv[...], ((0,), (0,)))
        out[at, :] = (total + dot(ggate[:, at], wg[...], ((0,), (0,)))).astype(BF16)

    spans(packed.shape[1], TILE, step)


def body(
    block_in,
    cotangent,
    segments,
    w_query,
    w_key,
    w_value,
    w_gate,
    w_out,
    w_up,
    w_down,
    retention_norm_gain,
    retention_norm_bias,
    feedforward_norm_gain,
    feedforward_norm_bias,
):
    depth = lax.axis_size("z")
    part = block_in.shape[1]
    width = 4 * part
    own = lax.axis_index(GROUP)
    plane = lax.axis_index("z")
    tokens = block_in.shape[0] // 4
    seq = 8 * tokens

    kq = w_query.shape[1] // HEADS
    kv = w_value.shape[1] // HEADS
    order_q = head_order(w_query.shape[1])
    order_v = head_order(w_value.shape[1])

    def by_head(weight, order):
        return dot(order, weight, ((0,), (1,))).astype(BF16).reshape(HEADS, -1, part)

    def to_heads(send):
        got = lax.all_to_all(send, GROUP, split_axis=0, concat_axis=0, tiled=True)
        got = got.reshape(4, 2, send.shape[1], part).transpose(1, 2, 0, 3)
        return got.reshape(2, send.shape[1], width)

    split = 2 if kq % 16 == 0 else 1
    blocks = depth * split

    def regroup(rows, *counts):
        if split == 2:
            return rows.reshape(-1, width)
        cuts = np.cumsum((0,) + counts)
        return jnp.concatenate(
            [rows[:, cuts[i] : cuts[i + 1]].reshape(-1, width) for i in range(len(counts))]
        )

    def ungroup(rows, *counts):
        if split == 2:
            return rows.reshape(2, -1, width)
        cuts = 2 * np.cumsum((0,) + counts)
        return jnp.concatenate(
            [rows[cuts[i] : cuts[i + 1]].reshape(2, -1, width) for i in range(len(counts))], axis=1
        )

    def planes(mine):
        return lax.all_gather(mine, "z", axis=0, tiled=True)

    got_qk = to_heads(
        jnp.concatenate([by_head(w_query, order_q), by_head(w_key, order_q)], axis=1)
    )
    mine_qk = regroup(got_qk, kq, kq)
    all_qk = planes(mine_qk)
    send_vgo = jnp.concatenate(
        [
            by_head(w_value, order_v),
            by_head(w_gate, order_v),
            dot(order_v, w_out, ((0,), (0,))).astype(BF16).reshape(HEADS, -1, part),
        ],
        axis=1,
    )
    got_vgo = to_heads(after(send_vgo, mine_qk))
    mine_vgo = regroup(got_vgo, kv, kv, kv)
    all_vgo = planes(mine_vgo)

    small = jnp.concatenate(
        [
            retention_norm_gain,
            retention_norm_bias,
            feedforward_norm_gain,
            feedforward_norm_bias,
            segments.astype(F32),
        ]
    )
    small = row_gather(after(small, mine_qk))
    params = small[:, : 4 * part].reshape(4, 4, part).transpose(1, 0, 2).reshape(4, width)
    segs = small[:, 4 * part :].astype(jnp.int32).reshape(depth, 8, tokens)
    block_in, cotangent = after(block_in, got_vgo), after(cotangent, got_vgo)
    stream_low, cot_own = to_wide(block_in, cotangent)
    mine_up, mine_down = to_wide(after(w_up, stream_low).T, after(w_down, stream_low))
    all_ud = planes(after(jnp.concatenate([mine_up, mine_down], axis=0), mine_vgo))
    stream = stream_low.astype(F32)
    hat_one, inv_one, norm_one = layernorm(stream, params[0], params[1])
    x_one = jnp.concatenate(group_gather(norm_one), axis=0)

    ids = lax.iota(jnp.int32, 8) ^ own
    ids = (ids % 2) * 4 + ids // 2
    picked = (ids[:, None] == lax.iota(jnp.int32, 8)[None, :])[:, :, None]
    here = (lax.iota(jnp.int32, depth) == plane)[:, None, None]
    seg_plane = jnp.sum(jnp.where(here, segs, 0), axis=0)
    seg = jnp.sum(jnp.where(picked, seg_plane[None], 0), axis=1).reshape(seq)
    pos = (ids[:, None] * tokens + lax.iota(jnp.int32, tokens)[None, :]).reshape(seq)

    loggam = jnp.log1p(-jnp.exp2(-5.0 - own.astype(F32)))
    lag = (pos - seq // 2).astype(F32) * loggam
    grow = jnp.exp(lag) * np.float32((kq * 2 * depth) ** (-0.5))
    where = (pos[:, None], pos[None, :], seg[:, None], seg[None, :])
    where = where + (grow[:, None], jnp.exp(-lag)[None, :])

    x_one = after(x_one, mine_up, mine_down)
    keys_all, values_all = kq * 2 * depth, kv * 2 * depth
    square = 2 * seq * seq
    qkv_shape = (2 * keys_all + values_all, width)
    query, keys, weights = kernel_call(
        functools.partial(retention_scores, blocks),
        [((keys_all, seq), BF16), ((keys_all, seq), BF16), ((seq, seq), BF16)],
        [],
        2 * seq * width * all_qk.shape[0] + square * keys_all,
        all_qk,
        x_one,
        *where,
    )
    cot = group_gather(after(cot_own, x_one))
    wide = 2 * seq * width * values_all
    narrow, broad = ((values_all, seq), BF16), ((values_all, width), BF16)
    plain = ((values_all, seq), F32)
    gate, hidden, attn, values, normed, inv_group = kernel_call(
        functools.partial(gated_forward, blocks),
        [plain, narrow, ((seq, width), BF16), narrow, plain, ((1, seq), F32)],
        [broad, broad, broad],
        3 * wide + square * values_all,
        all_vgo,
        x_one,
        after(weights, cot),
    )
    middle = stream + group_reduce(attn)

    hat_two, inv_two, norm_two = layernorm(middle, params[2], params[3])
    x_two = group_gather(norm_two)
    token = swap(after(norm_two[:8, :128], all_ud), 2)
    hidden_all = all_ud.shape[0] // 2
    wide_ff = 2 * seq * width * hidden_all
    narrow, broad = ((hidden_all, seq), BF16), ((hidden_all, width), BF16)
    tall = ((seq, width), BF16)
    act, two_part, full_ud = kernel_call(
        functools.partial(feedforward, depth),
        [narrow, tall, (all_ud.shape, BF16)],
        [broad, broad, tall, tall, narrow, narrow, ((seq, hidden_all), BF16), tall, broad, broad],
        5 * wide_ff,
        all_ud,
        *x_two,
        after(cot[0], token),
        *cot[1:],
        copies=4 * depth + 17 + width // WIDE,
    )
    grad_two = group_reduce(two_part)

    def home(full):
        return lax.psum_scatter(full, "z", scatter_dimension=0, tiled=True)

    def from_units(mine):
        send = mine.reshape(-1, 4, part).transpose(1, 0, 2)
        return row_exchange(send).reshape(-1, part)

    home_ud = home(full_ud)

    back_two, grad_ffn_gain, grad_ffn_bias = layernorm_back(grad_two, hat_two, inv_two, params[2])
    grad_mid = cot_own.astype(F32) + back_two
    x_mid = group_gather(grad_mid.astype(BF16))

    narrow, broad = ((values_all, seq), BF16), ((values_all, width), BF16)
    plain = ((values_all, seq), F32)
    grad_gate, grad_ret, full_go = kernel_call(
        functools.partial(gated_backward, blocks),
        [narrow, narrow, ((2 * values_all, width), BF16)],
        [broad, tall, tall, plain, plain, ((1, seq), F32), narrow, narrow, narrow, broad, broad],
        3 * wide,
        all_vgo,
        x_one,
        *x_mid,
        gate,
        normed,
        inv_group,
        hidden,
        copies=3 * blocks + 15,
    )
    home_go = home(full_go)
    home_shape = (depth, 8, 2 * kq + kv, part) if split == 2 else qkv_shape
    grad_qkv, full_qkv = kernel_call(
        functools.partial(retention_backward, blocks),
        [((qkv_shape[0], seq), BF16), (home_shape, BF16)],
        [((seq, seq), BF16)],
        2 * seq * width * qkv_shape[0] + 2 * square * (keys_all + values_all),
        query,
        keys,
        values,
        weights,
        grad_ret,
        x_one,
        *where,
    )
    home_qkv = home(full_qkv)
    half = home_ud.shape[0] // 2
    grad_up, grad_down = from_wide(home_ud[:half], home_ud[half:])
    (one_part,) = kernel_call(
        functools.partial(input_backward, blocks),
        [((seq, width), BF16)],
        [broad, broad],
        2 * seq * width * qkv_shape[0] + wide,
        grad_qkv,
        all_qk,
        after(grad_gate, full_qkv, grad_up),
        all_vgo,
    )
    grad_one = group_reduce(one_part)
    (ffn_part,) = kernel_call(
        functools.partial(down_forward, depth),
        [((seq, width), BF16)],
        [((hidden_all, width), BF16)],
        wide_ff,
        all_ud,
        after(act, one_part),
    )
    ffn = group_reduce(ffn_part)
    back_one, grad_attn_gain, grad_attn_bias = layernorm_back(grad_one, hat_one, inv_one, params[0])
    totals = total_over_all(
        jnp.stack([grad_attn_gain, grad_attn_bias, grad_ffn_gain, grad_ffn_bias])
    )
    totals = lax.dynamic_slice_in_dim(totals, lax.axis_index(ROW) * part, part, 1)
    grad_in, block_out = from_wide(
        (grad_mid + back_one).astype(BF16), (middle + ffn).astype(BF16)
    )
    grad_in = grad_in.astype(F32)

    def from_heads(mine):
        send = mine.reshape(2, -1, 4, part).transpose(2, 0, 1, 3).reshape(8, -1, part)
        return lax.all_to_all(send, GROUP, split_axis=0, concat_axis=0, tiled=True)

    def columns(grads, order):
        return dot(grads.reshape(-1, part), order, ((0,), (1,)))

    go = from_heads(ungroup(after(home_go, grad_in), kv, kv))
    home_qkv = after(home_qkv, go, totals)
    if split == 2:
        home_qkv = home_qkv.reshape(8, 2 * kq + kv, part)
        back = lax.all_to_all(home_qkv, GROUP, split_axis=0, concat_axis=0, tiled=True)
    else:
        back = from_heads(ungroup(home_qkv, kq, kq, kv))
    grad_up, grad_down = grad_up.T.astype(F32), grad_down.astype(F32)
    out_gate = columns(go[:, :kv], order_v)
    out_out = dot(order_v, go[:, kv:].reshape(-1, part), ((1,), (0,)))
    out_query = columns(back[:, :kq], order_q)
    out_key = columns(back[:, kq : 2 * kq], order_q)
    out_value = columns(back[:, 2 * kq :], order_v)
    return (
        block_out,
        grad_in,
        out_query,
        out_key,
        out_value,
        out_gate,
        out_out,
        grad_up,
        grad_down,
        totals[0],
        totals[1],
        totals[2],
        totals[3],
    )


def solution(mesh):
    rows, cols = mesh.devices.shape
    fine = Mesh(mesh.devices.reshape(rows // 2, 2, cols // 2, 2), ("x", "k", "z", "y"))
    row, col = ("x", "k"), ("z", "y")
    tok, unit = P(col, row), P(row, col)
    return jax.shard_map(
        body,
        mesh=fine,
        in_specs=(tok, tok, P(row), unit, unit, unit, unit, tok, unit, tok)
        + (P(row),) * 4,
        out_specs=(tok, tok, unit, unit, unit, unit, tok, unit, tok) + (P(row),) * 4,
        check_vma=False,
    )
```

```python
import functools
import math

import jax
import jax.numpy as jnp
import numpy as np
from jax import lax
from jax.experimental import pallas as pl
from jax.experimental.pallas import tpu as pltpu
from jax.sharding import Mesh
from jax.sharding import PartitionSpec as P

HEADS = 8
EPS_NORM = 1e-05
EPS_GROUP = 0.25

ROW = ("x", "k")
GROUP = ("x", "k", "y")
EVERY = ("x", "k", "z", "y")
F32 = jnp.float32
BF16 = jnp.bfloat16


def dot(left, right, over):
    return lax.dot_general(left, right, (over, ((), ())), preferred_element_type=F32)


def swap(value, mask):
    return lax.ppermute(value, GROUP, [(i, i ^ mask) for i in range(8)])


def group_gather(part, *others):
    near = [part, swap(part, 1), swap(part, 4), swap(part, 5)]
    far = [swap(after(block, *others), 2) for block in near]
    return near[:2] + far[:2] + near[2:] + far[2:]


def reduce_pairs(total):
    height = total.shape[0] // 8

    def pair(j):
        kept = total[j * height : (j + 1) * height]
        return kept.astype(F32) + swap(total[(j + 2) * height : (j + 3) * height], 2).astype(F32)

    return pair(5).astype(BF16), pair(4), pair(1), pair(0)


def reduce_relay(state):
    across, over_x, over_y, own = state
    half = across.shape[0] // 2
    top, low = swap(across[:half], 1).astype(F32), swap(across[half:], 4).astype(F32)
    over_x = jnp.concatenate([over_x[:half] + top, over_x[half:]], axis=0).astype(BF16)
    over_y = jnp.concatenate([over_y[:half], over_y[half:] + low], axis=0).astype(BF16)
    return over_x, over_y, own


def reduce_last(state):
    over_x, over_y, own = state
    return own + swap(over_x, 4).astype(F32) + swap(over_y, 1).astype(F32)


def group_reduce(total):
    return reduce_last(reduce_relay(reduce_pairs(total)))


def after(value, *others):
    return lax.optimization_barrier((value,) + others)[0]


def total_over_all(value):
    value = value + swap(value, 2)
    value = value + swap(value, 1) + swap(value, 4) + swap(value, 5)
    depth = lax.axis_size("z")
    if depth > 4:
        return lax.psum(value, "z")
    own = value
    for step in range(1, depth):
        value = value + lax.ppermute(own, "z", [(i, (i + step) % depth) for i in range(depth)])
    return value


def row_gather(value):
    got = [value, swap(value, 2), swap(value, 4), swap(value, 6)]
    own = lax.axis_index(ROW)
    rows = []
    for i in range(4):
        picks = [jnp.where((own ^ j) == i, got[j], 0.0) for j in range(4)]
        rows.append(picks[0] + picks[1] + picks[2] + picks[3])
    return jnp.stack(rows)


def row_exchange(parts):
    return lax.all_to_all(parts, ROW, split_axis=0, concat_axis=0, tiled=True)


def to_wide(*parts):
    height, width = parts[0].shape
    moved = row_exchange(jnp.stack([p.reshape(4, -1, width) for p in parts], axis=1))
    moved = moved.transpose(1, 2, 0, 3).reshape(len(parts), height // 4, 4 * width)
    return [moved[i] for i in range(len(parts))]


def from_wide(*parts):
    height, width = parts[0].shape
    moved = row_exchange(
        jnp.stack(parts).reshape(len(parts), height, 4, width // 4).transpose(2, 0, 1, 3)
    )
    moved = moved.transpose(1, 0, 2, 3).reshape(len(parts), 4 * height, width // 4)
    return [moved[i] for i in range(len(parts))]


def head_order(count):
    units = count // HEADS
    j = lax.iota(jnp.int32, count)
    target = (j % HEADS) * units + j // HEADS
    return (target[:, None] == lax.iota(jnp.int32, count)[None, :]).astype(BF16)


def layernorm(value, gain, bias):
    mean = jnp.mean(value, axis=1, keepdims=True)
    centered = value - mean
    inverse = lax.rsqrt(jnp.mean(centered * centered, axis=1, keepdims=True) + EPS_NORM)
    hat = centered * inverse
    return hat, inverse, (hat * gain + bias).astype(BF16)


def layernorm_back(grad, hat, inverse, gain):
    scaled = grad * gain
    first = jnp.mean(scaled, axis=1, keepdims=True)
    second = jnp.mean(scaled * hat, axis=1, keepdims=True)
    return (
        inverse * (scaled - first - hat * second),
        jnp.sum(grad * hat, axis=0),
        jnp.sum(grad, axis=0),
    )


TILE = 256
WIDE = 512
TALL = 512
LIMIT = 58 * 1024 * 1024


def spans(total, tile, step):
    def once(i, carry):
        step(pl.ds(pl.multiple_of(i * tile, tile), tile))
        return carry

    lax.fori_loop(0, total // tile, once, 0)


def kernel_call(body, outs, scratch, flops, *args, copies=0):
    moved = sum(a.size * a.dtype.itemsize for a in args)
    moved += sum(math.prod(shape) * jnp.dtype(kind).itemsize for shape, kind in outs)
    whole = pl.BlockSpec(memory_space=pl.ANY if copies else pltpu.VMEM)
    return pl.pallas_call(
        body,
        out_shape=[jax.ShapeDtypeStruct(shape, kind) for shape, kind in outs],
        in_specs=[whole] * len(args),
        out_specs=[whole] * len(outs),
        scratch_shapes=[pltpu.VMEM(shape, kind) for shape, kind in scratch]
        + [pltpu.SemaphoreType.DMA((copies,))] * bool(copies),
        compiler_params=pltpu.CompilerParams(vmem_limit_bytes=LIMIT),
        cost_estimate=pl.CostEstimate(flops=flops, bytes_accessed=moved, transcendentals=0),
    )(*args)


def unpack(source, targets, depth):
    height = source.shape[0] // (len(targets) * depth)
    for i in range(depth):
        for j, target in enumerate(targets):
            at = (i * len(targets) + j) * height
            if target is not None:
                target[i * height : (i + 1) * height, :] = source[at : at + height, :]


def decayed(raw, spot, segs, grow, fall, rows):
    inside = (spot[0][rows, :] >= spot[1][...]) & (segs[0][rows, :] == segs[1][...])
    return jnp.where(inside, raw * (grow[rows, :] * fall[...]), 0.0).astype(BF16)


def retention_scores(depth, w, x, pc, pr, sc, sr, grow, fall, q, k, weights):
    seq = x.shape[0]
    part = q.shape[0] // depth

    def project(at):
        out = dot(w[...], x[at, :], ((1,), (1,))).astype(BF16)
        for i in range(depth):
            z = 2 * i * part
            q[i * part : (i + 1) * part, at] = out[z : z + part]
            k[i * part : (i + 1) * part, at] = out[z + part : z + 2 * part]

    def attend(at):
        raw = dot(q[:, at], k[...], ((0,), (0,)))
        weights[at, :] = decayed(raw, (pc, pr), (sc, sr), grow, fall, at)

    spans(seq, TILE, project)
    spans(seq, TILE, attend)


def gated_forward(depth, w, x, weights, gate, hidden, out, v, normed, inv, wv, wg, wo):
    unpack(w, (wv, wg, wo), depth)

    def project(at):
        v[:, at] = dot(wv[...], x[at, :], ((1,), (1,))).astype(BF16)

    def step(at):
        kept = dot(v[...], weights[at, :], ((1,), (1,)))
        centered = kept - jnp.mean(kept, axis=0, keepdims=True)
        scale = lax.rsqrt(jnp.mean(centered * centered, axis=0, keepdims=True) + EPS_GROUP)
        full = centered * scale
        normed[:, at] = full
        inv[:, at] = scale
        g = dot(wg[...], x[at, :], ((1,), (1,)))
        gate[:, at] = g
        h = (g * jax.nn.sigmoid(g) * full.astype(BF16).astype(F32)).astype(BF16)
        hidden[:, at] = h
        out[at, :] = dot(h, wo[...], ((0,), (0,))).astype(BF16)

    spans(x.shape[0], TILE, project)
    spans(x.shape[0], TILE, step)


class Mover:
    def __init__(self, semaphores):
        self.semaphores = semaphores
        self.count = 0

    def start(self, source, target):
        copy = pltpu.make_async_copy(source, target, self.semaphores.at[self.count])
        self.count += 1
        copy.start()
        return copy

    def rows(self, sources, target):
        height = sources[0].shape[0]
        return [
            self.start(source, target.at[pl.ds(i * height, height)])
            for i, source in enumerate(sources)
        ]

    def kind(self, source, target, which, depth):
        way, index, kinds = which
        height = (source if way == "from" else target).shape[0] // (kinds * depth)
        moved = []
        for i in range(depth):
            mixed = pl.ds((kinds * i + index) * height, height)
            plain = pl.ds(i * height, height)
            if way == "from":
                moved.append(self.start(source.at[mixed], target.at[plain]))
            else:
                moved.append(self.start(source.at[plain], target.at[mixed]))
        return moved


def wait(copies):
    for copy in copies:
        copy.wait()


def feedforward(depth, w, *refs):
    x_blocks, cot_blocks = refs[:8], refs[8:16]
    act_out, back_out, grads_out = refs[16:19]
    wu, wd, x, cot, act, gp, turned, back, gu, gd, semaphores = refs[19:]
    move = Mover(semaphores)
    seq, rows = x.shape[0], x_blocks[0].shape[0]
    first = TALL // rows
    wu_copies = move.kind(w, wu, ("from", 0, 2), depth)
    x_copies = move.rows(x_blocks[:first], x.at[pl.ds(0, TALL)])
    wd_copies = move.kind(w, wd, ("from", 1, 2), depth)
    cot_copies = move.rows(cot_blocks[:first], cot.at[pl.ds(0, TALL)])
    x_copies += move.rows(x_blocks[first:], x.at[pl.ds(TALL, seq - TALL)])
    cot_copies += move.rows(cot_blocks[first:], cot.at[pl.ds(TALL, seq - TALL)])
    wait(wu_copies + x_copies + wd_copies + cot_copies)

    def step(at):
        pre = dot(wu[...], x[at, :], ((1,), (1,)))
        grad = dot(wd[...], cot[at, :], ((1,), (1,)))
        half = 0.5 * (1.0 + lax.erf(pre * np.float32(0.5**0.5)))
        act[:, at] = (pre * half).astype(BF16)
        bell = jnp.exp(-0.5 * pre * pre) * np.float32((2 * math.pi) ** -0.5)
        low = grad * (half + pre * bell)
        gp[:, at] = low.astype(BF16)
        turned[at, :] = low.T.astype(BF16)

    spans(seq, TALL, step)
    sent = [move.start(act, act_out)]

    def up_step(at):
        gu[:, at] = dot(gp[...], x[:, at], ((1,), (0,))).astype(BF16)

    def down_step(at):
        gd[:, at] = dot(act[...], cot[:, at], ((1,), (0,))).astype(BF16)

    spans(x.shape[1], WIDE, up_step)
    sent += move.kind(gu, grads_out, ("to", 0, 2), depth)
    spans(x.shape[1], WIDE, down_step)
    sent += move.kind(gd, grads_out, ("to", 1, 2), depth)
    def back_step(at):
        back[:, at] = dot(turned[...], wu[:, at], ((1,), (0,))).astype(BF16)

    spans(x.shape[1], WIDE, back_step)
    sent.append(move.start(back, back_out))
    wait(sent)


def down_forward(depth, w, act, out, wd):
    unpack(w, (None, wd), depth)

    def step(at):
        out[at, :] = dot(act[:, at], wd[...], ((0,), (0,))).astype(BF16)

    spans(act.shape[1], TILE, step)


def gated_backward(depth, w, x_in, *refs):
    mid_blocks = refs[:8]
    gate_in, normed_in, inv_in, hidden_in, ggate_out, gret_out, grads_out = refs[8:15]
    wo, x, mid, gate, normed, inv, hidden, ggate, gret, gg, go, semaphores = refs[15:]
    move = Mover(semaphores)
    seq, rows = x.shape[0], mid_blocks[0].shape[0]
    first = move.kind(w, wo, ("from", 2, 3), depth)
    mid_copies = move.rows(mid_blocks[:4], mid.at[pl.ds(0, 4 * rows)])
    second = [move.start(inv_in, inv), move.start(gate_in, gate), move.start(normed_in, normed)]
    mid_copies += move.rows(mid_blocks[4:], mid.at[pl.ds(4 * rows, seq - 4 * rows)])
    late = [move.start(x_in, x), move.start(hidden_in, hidden)]
    wait(first)
    for tile in range(seq // TALL):
        wait(mid_copies[tile * TALL // rows : (tile + 1) * TALL // rows])
        at = pl.ds(tile * TALL, TALL)
        up = dot(wo[...], mid[at, :], ((1,), (1,)))
        if tile == 0:
            wait(second)
        g = gate[:, at]
        s = jax.nn.sigmoid(g)
        full = normed[:, at]
        low = full.astype(BF16).astype(F32)
        ggate[:, at] = (up * low * (s * (1.0 + g * (1.0 - s)))).astype(BF16)
        gn = (up * (g * s)).astype(BF16).astype(F32)
        mean = jnp.mean(gn, axis=0, keepdims=True)
        slope = jnp.mean(gn * full, axis=0, keepdims=True)
        gret[:, at] = (inv[:, at] * (gn - mean - full * slope)).astype(BF16)
    sent = [move.start(ggate, ggate_out), move.start(gret, gret_out)]
    wait(late)

    def gate_step(at):
        gg[:, at] = dot(ggate[...], x[:, at], ((1,), (0,))).astype(BF16)

    def out_step(at):
        go[:, at] = dot(hidden[...], mid[:, at], ((1,), (0,))).astype(BF16)

    spans(x.shape[1], WIDE, gate_step)
    sent += move.kind(gg, grads_out, ("to", 0, 2), depth)
    spans(x.shape[1], WIDE, out_step)
    sent += move.kind(go, grads_out, ("to", 1, 2), depth)
    wait(sent)


def retention_backward(
    depth, q, k, v, weights, gret, x, pc, pr, sc, sr, grow, fall, packed, grads, scores
):
    seq = x.shape[0]
    part = q.shape[0] // depth
    width = v.shape[0] // depth
    pairs = 2 * part * depth

    def place(value, at, offset):
        for i in range(depth):
            z = 2 * i * part + offset
            packed[z : z + part, at] = value[i * part : (i + 1) * part]

    def query_step(at):
        raw = dot(gret[:, at], v[...], ((0,), (0,)))
        low = decayed(raw, (pc, pr), (sc, sr), grow, fall, at)
        scores[at, :] = low
        place(dot(k[...], low, ((1,), (1,))).astype(BF16), at, 0)

    def key_step(at):
        place(dot(q[...], scores[:, at], ((1,), (0,))).astype(BF16), at, part)
        packed[pairs:, at] = dot(gret[...], weights[:, at], ((1,), (0,))).astype(BF16)

    spans(seq, TILE, query_step)
    spans(seq, TILE, key_step)
    if len(grads.shape) == 2:

        def grad_step(at):
            full = dot(packed[...], x[:, at], ((1,), (0,))).astype(BF16)
            for i in range(depth):
                z = i * (2 * part + width)
                grads[z : z + 2 * part, at] = full[2 * i * part : 2 * (i + 1) * part]
                grads[z + 2 * part : z + 2 * part + width, at] = full[
                    pairs + i * width : pairs + (i + 1) * width
                ]

        spans(x.shape[1], WIDE, grad_step)
        return

    def home_step(row, carry):
        columns = grads.shape[3]
        at = pl.ds(pl.multiple_of(row * columns, columns), columns)
        full = dot(packed[...], x[:, at], ((1,), (0,))).astype(BF16)
        for i in range(depth):
            there = (i // 2, 2 * row + i % 2)
            grads[(*there, slice(0, 2 * part))] = full[2 * i * part : 2 * (i + 1) * part]
            grads[(*there, slice(2 * part, 2 * part + width))] = full[
                pairs + i * width : pairs + (i + 1) * width
            ]
        return carry

    lax.fori_loop(0, 4, home_step, 0)


def input_backward(depth, packed, w, ggate, vgo, out, wv, wg):
    unpack(vgo, (wv, wg, None), depth)
    pairs = w.shape[0]

    def step(at):
        total = dot(packed[:pairs, at], w[...], ((0,), (0,)))
        total = total + dot(packed[pairs:, at], wv[...], ((0,), (0,)))
        out[at, :] = (total + dot(ggate[:, at], wg[...], ((0,), (0,)))).astype(BF16)

    spans(packed.shape[1], TILE, step)


def body(
    block_in,
    cotangent,
    segments,
    w_query,
    w_key,
    w_value,
    w_gate,
    w_out,
    w_up,
    w_down,
    retention_norm_gain,
    retention_norm_bias,
    feedforward_norm_gain,
    feedforward_norm_bias,
):
    depth = lax.axis_size("z")
    part = block_in.shape[1]
    width = 4 * part
    own = lax.axis_index(GROUP)
    plane = lax.axis_index("z")
    tokens = block_in.shape[0] // 4
    seq = 8 * tokens

    kq = w_query.shape[1] // HEADS
    kv = w_value.shape[1] // HEADS
    order_q = head_order(w_query.shape[1])
    order_v = head_order(w_value.shape[1])

    def by_head(weight, order):
        return dot(order, weight, ((0,), (1,))).astype(BF16).reshape(HEADS, -1, part)

    def to_heads(send):
        got = lax.all_to_all(send, GROUP, split_axis=0, concat_axis=0, tiled=True)
        got = got.reshape(4, 2, send.shape[1], part).transpose(1, 2, 0, 3)
        return got.reshape(2, send.shape[1], width)

    split = 2 if kq % 16 == 0 else 1
    blocks = depth * split

    def regroup(rows, *counts):
        if split == 2:
            return rows.reshape(-1, width)
        cuts = np.cumsum((0,) + counts)
        return jnp.concatenate(
            [rows[:, cuts[i] : cuts[i + 1]].reshape(-1, width) for i in range(len(counts))]
        )

    def ungroup(rows, *counts):
        if split == 2:
            return rows.reshape(2, -1, width)
        cuts = 2 * np.cumsum((0,) + counts)
        return jnp.concatenate(
            [rows[cuts[i] : cuts[i + 1]].reshape(2, -1, width) for i in range(len(counts))], axis=1
        )

    def planes(mine):
        return lax.all_gather(mine, "z", axis=0, tiled=True)

    send_qk = jnp.concatenate([by_head(w_query, order_q), by_head(w_key, order_q)], axis=1)
    from_planes = planes(send_qk.reshape(-1, part)).reshape(depth, HEADS, -1, part)
    send_vgo = jnp.concatenate(
        [
            by_head(w_value, order_v),
            by_head(w_gate, order_v),
            dot(order_v, w_out, ((0,), (0,))).astype(BF16).reshape(HEADS, -1, part),
        ],
        axis=1,
    )
    got_vgo = to_heads(after(send_vgo, send_qk))
    mine_vgo = regroup(got_vgo, kv, kv, kv)
    all_vgo = planes(mine_vgo)

    small = jnp.concatenate(
        [
            retention_norm_gain,
            retention_norm_bias,
            feedforward_norm_gain,
            feedforward_norm_bias,
            segments.astype(F32),
        ]
    )
    small = row_gather(after(small, send_qk))
    params = small[:, : 4 * part].reshape(4, 4, part).transpose(1, 0, 2).reshape(4, width)
    segs = small[:, 4 * part :].astype(jnp.int32).reshape(depth, 8, tokens)
    block_in, cotangent = after(block_in, got_vgo), after(cotangent, got_vgo)
    stream_low, cot_own = to_wide(block_in, cotangent)
    mine_up, mine_down = to_wide(after(w_up, stream_low).T, after(w_down, stream_low))
    all_ud = planes(after(jnp.concatenate([mine_up, mine_down], axis=0), mine_vgo))
    stream = stream_low.astype(F32)
    hat_one, inv_one, norm_one = layernorm(stream, params[0], params[1])
    x_one = jnp.concatenate(group_gather(norm_one), axis=0)

    ids = lax.iota(jnp.int32, 8) ^ own
    ids = (ids % 2) * 4 + ids // 2
    picked = (ids[:, None] == lax.iota(jnp.int32, 8)[None, :])[:, :, None]
    here = (lax.iota(jnp.int32, depth) == plane)[:, None, None]
    seg_plane = jnp.sum(jnp.where(here, segs, 0), axis=0)
    seg = jnp.sum(jnp.where(picked, seg_plane[None], 0), axis=1).reshape(seq)
    pos = (ids[:, None] * tokens + lax.iota(jnp.int32, tokens)[None, :]).reshape(seq)

    loggam = jnp.log1p(-jnp.exp2(-5.0 - own.astype(F32)))
    lag = (pos - seq // 2).astype(F32) * loggam
    grow = jnp.exp(lag) * np.float32((kq * 2 * depth) ** (-0.5))
    where = (pos[:, None], pos[None, :], seg[:, None], seg[None, :])
    where = where + (grow[:, None], jnp.exp(-lag)[None, :])

    got_qk = lax.all_to_all(
        from_planes.transpose(1, 0, 2, 3), GROUP, split_axis=0, concat_axis=0, tiled=True
    ).reshape(4, 2, depth, 2, kq, part)
    order = (2, 1, 3, 4, 0, 5) if split == 2 else (2, 3, 1, 4, 0, 5)
    all_qk = got_qk.transpose(order).reshape(-1, width)
    x_one = after(x_one, mine_up, mine_down)
    keys_all, values_all = kq * 2 * depth, kv * 2 * depth
    square = 2 * seq * seq
    qkv_shape = (2 * keys_all + values_all, width)
    query, keys, weights = kernel_call(
        functools.partial(retention_scores, blocks),
        [((keys_all, seq), BF16), ((keys_all, seq), BF16), ((seq, seq), BF16)],
        [],
        2 * seq * width * all_qk.shape[0] + square * keys_all,
        all_qk,
        x_one,
        *where,
    )
    cot = group_gather(after(cot_own, x_one))
    wide = 2 * seq * width * values_all
    narrow, broad = ((values_all, seq), BF16), ((values_all, width), BF16)
    plain = ((values_all, seq), F32)
    gate, hidden, attn, values, normed, inv_group = kernel_call(
        functools.partial(gated_forward, blocks),
        [plain, narrow, ((seq, width), BF16), narrow, plain, ((1, seq), F32)],
        [broad, broad, broad],
        3 * wide + square * values_all,
        all_vgo,
        x_one,
        after(weights, cot),
    )
    middle = stream + group_reduce(attn)

    hat_two, inv_two, norm_two = layernorm(middle, params[2], params[3])
    x_two = group_gather(norm_two)
    token = swap(after(norm_two[:8, :128], all_ud), 2)
    hidden_all = all_ud.shape[0] // 2
    wide_ff = 2 * seq * width * hidden_all
    narrow, broad = ((hidden_all, seq), BF16), ((hidden_all, width), BF16)
    tall = ((seq, width), BF16)
    act, two_part, full_ud = kernel_call(
        functools.partial(feedforward, depth),
        [narrow, tall, (all_ud.shape, BF16)],
        [broad, broad, tall, tall, narrow, narrow, ((seq, hidden_all), BF16), tall, broad, broad],
        5 * wide_ff,
        all_ud,
        *x_two,
        after(cot[0], token),
        *cot[1:],
        copies=4 * depth + 18,
    )
    grad_two = group_reduce(two_part)

    def home(full):
        return lax.psum_scatter(full, "z", scatter_dimension=0, tiled=True)

    def from_units(mine):
        send = mine.reshape(-1, 4, part).transpose(1, 0, 2)
        return row_exchange(send).reshape(-1, part)

    home_ud = home(full_ud)

    back_two, grad_ffn_gain, grad_ffn_bias = layernorm_back(grad_two, hat_two, inv_two, params[2])
    grad_mid = cot_own.astype(F32) + back_two
    x_mid = group_gather(grad_mid.astype(BF16))

    narrow, broad = ((values_all, seq), BF16), ((values_all, width), BF16)
    plain = ((values_all, seq), F32)
    grad_gate, grad_ret, full_go = kernel_call(
        functools.partial(gated_backward, blocks),
        [narrow, narrow, ((2 * values_all, width), BF16)],
        [broad, tall, tall, plain, plain, ((1, seq), F32), narrow, narrow, narrow, broad, broad],
        3 * wide,
        all_vgo,
        x_one,
        *x_mid,
        gate,
        normed,
        inv_group,
        hidden,
        copies=3 * blocks + 15,
    )
    home_go = home(full_go)
    home_shape = (depth, 8, 2 * kq + kv, part) if split == 2 else qkv_shape
    grad_qkv, full_qkv = kernel_call(
        functools.partial(retention_backward, blocks),
        [((qkv_shape[0], seq), BF16), (home_shape, BF16)],
        [((seq, seq), BF16)],
        2 * seq * width * qkv_shape[0] + 2 * square * (keys_all + values_all),
        query,
        keys,
        values,
        weights,
        grad_ret,
        x_one,
        *where,
    )
    home_qkv = home(full_qkv)
    half = home_ud.shape[0] // 2
    grad_up, grad_down = from_wide(home_ud[:half], home_ud[half:])
    (one_part,) = kernel_call(
        functools.partial(input_backward, blocks),
        [((seq, width), BF16)],
        [broad, broad],
        2 * seq * width * qkv_shape[0] + wide,
        grad_qkv,
        all_qk,
        after(grad_gate, full_qkv, grad_up),
        all_vgo,
    )
    grad_one = group_reduce(one_part)
    (ffn_part,) = kernel_call(
        functools.partial(down_forward, depth),
        [((seq, width), BF16)],
        [((hidden_all, width), BF16)],
        wide_ff,
        all_ud,
        after(act, one_part),
    )
    ffn = group_reduce(ffn_part)
    back_one, grad_attn_gain, grad_attn_bias = layernorm_back(grad_one, hat_one, inv_one, params[0])
    totals = total_over_all(
        jnp.stack([grad_attn_gain, grad_attn_bias, grad_ffn_gain, grad_ffn_bias])
    )
    totals = lax.dynamic_slice_in_dim(totals, lax.axis_index(ROW) * part, part, 1)
    grad_in, block_out = from_wide(
        (grad_mid + back_one).astype(BF16), (middle + ffn).astype(BF16)
    )
    grad_in = grad_in.astype(F32)

    def from_heads(mine):
        send = mine.reshape(2, -1, 4, part).transpose(2, 0, 1, 3).reshape(8, -1, part)
        return lax.all_to_all(send, GROUP, split_axis=0, concat_axis=0, tiled=True)

    def columns(grads, order):
        return dot(grads.reshape(-1, part), order, ((0,), (1,)))

    go = from_heads(ungroup(after(home_go, grad_in), kv, kv))
    home_qkv = after(home_qkv, go, totals)
    if split == 2:
        home_qkv = home_qkv.reshape(8, 2 * kq + kv, part)
        back = lax.all_to_all(home_qkv, GROUP, split_axis=0, concat_axis=0, tiled=True)
    else:
        back = from_heads(ungroup(home_qkv, kq, kq, kv))
    grad_up, grad_down = grad_up.T.astype(F32), grad_down.astype(F32)
    out_gate = columns(go[:, :kv], order_v)
    out_out = dot(order_v, go[:, kv:].reshape(-1, part), ((1,), (0,)))
    out_query = columns(back[:, :kq], order_q)
    out_key = columns(back[:, kq : 2 * kq], order_q)
    out_value = columns(back[:, 2 * kq :], order_v)
    return (
        block_out,
        grad_in,
        out_query,
        out_key,
        out_value,
        out_gate,
        out_out,
        grad_up,
        grad_down,
        totals[0],
        totals[1],
        totals[2],
        totals[3],
    )


def solution(mesh):
    rows, cols = mesh.devices.shape
    fine = Mesh(mesh.devices.reshape(rows // 2, 2, cols // 2, 2), ("x", "k", "z", "y"))
    row, col = ("x", "k"), ("z", "y")
    tok, unit = P(col, row), P(row, col)
    return jax.shard_map(
        body,
        mesh=fine,
        in_specs=(tok, tok, P(row), unit, unit, unit, unit, tok, unit, tok)
        + (P(row),) * 4,
        out_specs=(tok, tok, unit, unit, unit, unit, tok, unit, tok) + (P(row),) * 4,
        check_vma=False,
    )
```

```python
import functools
import math

import jax
import jax.numpy as jnp
import numpy as np
from jax import lax
from jax.experimental import pallas as pl
from jax.experimental.pallas import tpu as pltpu
from jax.sharding import Mesh
from jax.sharding import PartitionSpec as P

HEADS = 8
EPS_NORM = 1e-05
EPS_GROUP = 0.25

ROW = ("x", "k")
GROUP = ("x", "k", "y")
EVERY = ("x", "k", "z", "y")
F32 = jnp.float32
BF16 = jnp.bfloat16


def dot(left, right, over):
    return lax.dot_general(left, right, (over, ((), ())), preferred_element_type=F32)


def swap(value, mask):
    return lax.ppermute(value, GROUP, [(i, i ^ mask) for i in range(8)])


def group_gather(part, *others):
    near = [part, swap(part, 1), swap(part, 4), swap(part, 5)]
    far = [swap(after(block, *others), 2) for block in near]
    return near[:2] + far[:2] + near[2:] + far[2:]


def reduce_pairs(total):
    height = total.shape[0] // 8

    def pair(j):
        kept = total[j * height : (j + 1) * height]
        return kept.astype(F32) + swap(total[(j + 2) * height : (j + 3) * height], 2).astype(F32)

    return pair(5).astype(BF16), pair(4), pair(1), pair(0)


def reduce_relay(state):
    across, over_x, over_y, own = state
    half = across.shape[0] // 2
    top, low = swap(across[:half], 1).astype(F32), swap(across[half:], 4).astype(F32)
    over_x = jnp.concatenate([over_x[:half] + top, over_x[half:]], axis=0).astype(BF16)
    over_y = jnp.concatenate([over_y[:half], over_y[half:] + low], axis=0).astype(BF16)
    return over_x, over_y, own


def reduce_last(state):
    over_x, over_y, own = state
    return own + swap(over_x, 4).astype(F32) + swap(over_y, 1).astype(F32)


def group_reduce(total):
    return reduce_last(reduce_relay(reduce_pairs(total)))


def after(value, *others):
    return lax.optimization_barrier((value,) + others)[0]


def total_over_all(value):
    value = value + swap(value, 2)
    value = value + swap(value, 1) + swap(value, 4) + swap(value, 5)
    depth = lax.axis_size("z")
    if depth > 4:
        return lax.psum(value, "z")
    own = value
    for step in range(1, depth):
        value = value + lax.ppermute(own, "z", [(i, (i + step) % depth) for i in range(depth)])
    return value


def row_gather(value):
    got = [value, swap(value, 2), swap(value, 4), swap(value, 6)]
    own = lax.axis_index(ROW)
    rows = []
    for i in range(4):
        picks = [jnp.where((own ^ j) == i, got[j], 0.0) for j in range(4)]
        rows.append(picks[0] + picks[1] + picks[2] + picks[3])
    return jnp.stack(rows)


def row_exchange(parts):
    return lax.all_to_all(parts, ROW, split_axis=0, concat_axis=0, tiled=True)


def to_wide(*parts):
    height, width = parts[0].shape
    moved = row_exchange(jnp.stack([p.reshape(4, -1, width) for p in parts], axis=1))
    moved = moved.transpose(1, 2, 0, 3).reshape(len(parts), height // 4, 4 * width)
    return [moved[i] for i in range(len(parts))]


def from_wide(*parts):
    height, width = parts[0].shape
    moved = row_exchange(
        jnp.stack(parts).reshape(len(parts), height, 4, width // 4).transpose(2, 0, 1, 3)
    )
    moved = moved.transpose(1, 0, 2, 3).reshape(len(parts), 4 * height, width // 4)
    return [moved[i] for i in range(len(parts))]


def head_order(count):
    units = count // HEADS
    j = lax.iota(jnp.int32, count)
    target = (j % HEADS) * units + j // HEADS
    return (target[:, None] == lax.iota(jnp.int32, count)[None, :]).astype(BF16)


def layernorm(value, gain, bias):
    mean = jnp.mean(value, axis=1, keepdims=True)
    centered = value - mean
    inverse = lax.rsqrt(jnp.mean(centered * centered, axis=1, keepdims=True) + EPS_NORM)
    hat = centered * inverse
    return hat, inverse, (hat * gain + bias).astype(BF16)


def layernorm_back(grad, hat, inverse, gain):
    scaled = grad * gain
    first = jnp.mean(scaled, axis=1, keepdims=True)
    second = jnp.mean(scaled * hat, axis=1, keepdims=True)
    return (
        inverse * (scaled - first - hat * second),
        jnp.sum(grad * hat, axis=0),
        jnp.sum(grad, axis=0),
    )


TILE = 256
WIDE = 512
TALL = 512
LIMIT = 58 * 1024 * 1024


def spans(total, tile, step):
    def once(i, carry):
        step(pl.ds(pl.multiple_of(i * tile, tile), tile))
        return carry

    lax.fori_loop(0, total // tile, once, 0)


def kernel_call(body, outs, scratch, flops, *args, copies=0):
    moved = sum(a.size * a.dtype.itemsize for a in args)
    moved += sum(math.prod(shape) * jnp.dtype(kind).itemsize for shape, kind in outs)
    whole = pl.BlockSpec(memory_space=pl.ANY if copies else pltpu.VMEM)
    return pl.pallas_call(
        body,
        out_shape=[jax.ShapeDtypeStruct(shape, kind) for shape, kind in outs],
        in_specs=[whole] * len(args),
        out_specs=[whole] * len(outs),
        scratch_shapes=[pltpu.VMEM(shape, kind) for shape, kind in scratch]
        + [pltpu.SemaphoreType.DMA((copies,))] * bool(copies),
        compiler_params=pltpu.CompilerParams(vmem_limit_bytes=LIMIT),
        cost_estimate=pl.CostEstimate(flops=flops, bytes_accessed=moved, transcendentals=0),
    )(*args)


def unpack(source, targets, depth):
    height = source.shape[0] // (len(targets) * depth)
    for i in range(depth):
        for j, target in enumerate(targets):
            at = (i * len(targets) + j) * height
            if target is not None:
                target[i * height : (i + 1) * height, :] = source[at : at + height, :]


def decayed(raw, spot, segs, grow, fall, rows):
    inside = (spot[0][rows, :] >= spot[1][...]) & (segs[0][rows, :] == segs[1][...])
    return jnp.where(inside, raw * (grow[rows, :] * fall[...]), 0.0).astype(BF16)


def retention_scores(depth, w, x, pc, pr, sc, sr, grow, fall, q, k, weights):
    seq = x.shape[0]
    part = q.shape[0] // depth

    def project(at):
        out = dot(w[...], x[at, :], ((1,), (1,))).astype(BF16)
        for i in range(depth):
            z = 2 * i * part
            q[i * part : (i + 1) * part, at] = out[z : z + part]
            k[i * part : (i + 1) * part, at] = out[z + part : z + 2 * part]

    def attend(at):
        raw = dot(q[:, at], k[...], ((0,), (0,)))
        weights[at, :] = decayed(raw, (pc, pr), (sc, sr), grow, fall, at)

    spans(seq, TILE, project)
    spans(seq, TILE, attend)


def gated_forward(depth, w, x, weights, gate, hidden, out, v, normed, inv, wv, wg, wo):
    unpack(w, (wv, wg, wo), depth)

    def project(at):
        v[:, at] = dot(wv[...], x[at, :], ((1,), (1,))).astype(BF16)

    def step(at):
        kept = dot(v[...], weights[at, :], ((1,), (1,)))
        centered = kept - jnp.mean(kept, axis=0, keepdims=True)
        scale = lax.rsqrt(jnp.mean(centered * centered, axis=0, keepdims=True) + EPS_GROUP)
        full = centered * scale
        normed[:, at] = full
        inv[:, at] = scale
        g = dot(wg[...], x[at, :], ((1,), (1,)))
        gate[:, at] = g
        h = (g * jax.nn.sigmoid(g) * full.astype(BF16).astype(F32)).astype(BF16)
        hidden[:, at] = h
        out[at, :] = dot(h, wo[...], ((0,), (0,))).astype(BF16)

    spans(x.shape[0], TILE, project)
    spans(x.shape[0], TILE, step)


class Mover:
    def __init__(self, semaphores):
        self.semaphores = semaphores
        self.count = 0

    def start(self, source, target):
        copy = pltpu.make_async_copy(source, target, self.semaphores.at[self.count])
        self.count += 1
        copy.start()
        return copy

    def rows(self, sources, target):
        height = sources[0].shape[0]
        return [
            self.start(source, target.at[pl.ds(i * height, height)])
            for i, source in enumerate(sources)
        ]

    def kind(self, source, target, which, depth):
        way, index, kinds = which
        height = (source if way == "from" else target).shape[0] // (kinds * depth)
        moved = []
        for i in range(depth):
            mixed = pl.ds((kinds * i + index) * height, height)
            plain = pl.ds(i * height, height)
            if way == "from":
                moved.append(self.start(source.at[mixed], target.at[plain]))
            else:
                moved.append(self.start(source.at[plain], target.at[mixed]))
        return moved


def wait(copies):
    for copy in copies:
        copy.wait()


def feedforward(depth, w, *refs):
    x_blocks, cot_blocks = refs[:8], refs[8:16]
    act_out, back_out, grads_out = refs[16:19]
    wu, wd, x, cot, act, gp, turned, back, gu, gd, semaphores = refs[19:]
    move = Mover(semaphores)
    seq, rows = x.shape[0], x_blocks[0].shape[0]
    first = TALL // rows
    wu_copies = move.kind(w, wu, ("from", 0, 2), depth)
    x_copies = move.rows(x_blocks[:first], x.at[pl.ds(0, TALL)])
    wd_copies = move.kind(w, wd, ("from", 1, 2), depth)
    cot_copies = move.rows(cot_blocks[:first], cot.at[pl.ds(0, TALL)])
    x_copies += move.rows(x_blocks[first:], x.at[pl.ds(TALL, seq - TALL)])
    cot_copies += move.rows(cot_blocks[first:], cot.at[pl.ds(TALL, seq - TALL)])
    wait(wu_copies + x_copies + wd_copies + cot_copies)

    def step(at):
        pre = dot(wu[...], x[at, :], ((1,), (1,)))
        grad = dot(wd[...], cot[at, :], ((1,), (1,)))
        half = 0.5 * (1.0 + lax.erf(pre * np.float32(0.5**0.5)))
        act[:, at] = (pre * half).astype(BF16)
        bell = jnp.exp(-0.5 * pre * pre) * np.float32((2 * math.pi) ** -0.5)
        low = grad * (half + pre * bell)
        gp[:, at] = low.astype(BF16)
        turned[at, :] = low.T.astype(BF16)

    spans(seq, TALL, step)
    sent = [move.start(act, act_out)]

    def up_step(at):
        gu[:, at] = dot(gp[...], x[:, at], ((1,), (0,))).astype(BF16)

    def down_step(at):
        gd[:, at] = dot(act[...], cot[:, at], ((1,), (0,))).astype(BF16)

    spans(x.shape[1], WIDE, up_step)
    sent += move.kind(gu, grads_out, ("to", 0, 2), depth)
    spans(x.shape[1], WIDE, down_step)
    sent += move.kind(gd, grads_out, ("to", 1, 2), depth)
    tiles, base = x.shape[1] // WIDE, move.count

    def back_copy(i, at):
        return pltpu.make_async_copy(
            back.at[:, at], back_out.at[:, at], semaphores.at[base + i]
        )

    def back_step(i, carry):
        at = pl.ds(pl.multiple_of(i * WIDE, WIDE), WIDE)
        back[:, at] = dot(turned[...], wu[:, at], ((1,), (0,))).astype(BF16)
        back_copy(i, at).start()
        return carry

    lax.fori_loop(0, tiles, back_step, 0)
    wait(sent + [back_copy(i, pl.ds(i * WIDE, WIDE)) for i in range(tiles)])


def down_forward(depth, w, act, out, wd):
    unpack(w, (None, wd), depth)

    def step(at):
        out[at, :] = dot(act[:, at], wd[...], ((0,), (0,))).astype(BF16)

    spans(act.shape[1], TILE, step)


def gated_backward(depth, w, x_in, *refs):
    mid_blocks = refs[:8]
    gate_in, normed_in, inv_in, hidden_in, ggate_out, gret_out, grads_out = refs[8:15]
    wo, x, mid, gate, normed, inv, hidden, ggate, gret, gg, go, semaphores = refs[15:]
    move = Mover(semaphores)
    seq, rows = x.shape[0], mid_blocks[0].shape[0]
    first = move.kind(w, wo, ("from", 2, 3), depth)
    mid_copies = move.rows(mid_blocks[:4], mid.at[pl.ds(0, 4 * rows)])
    second = [move.start(inv_in, inv), move.start(gate_in, gate), move.start(normed_in, normed)]
    mid_copies += move.rows(mid_blocks[4:], mid.at[pl.ds(4 * rows, seq - 4 * rows)])
    late = [move.start(x_in, x), move.start(hidden_in, hidden)]
    wait(first)
    for tile in range(seq // TALL):
        wait(mid_copies[tile * TALL // rows : (tile + 1) * TALL // rows])
        at = pl.ds(tile * TALL, TALL)
        up = dot(wo[...], mid[at, :], ((1,), (1,)))
        if tile == 0:
            wait(second)
        g = gate[:, at]
        s = jax.nn.sigmoid(g)
        full = normed[:, at]
        low = full.astype(BF16).astype(F32)
        ggate[:, at] = (up * low * (s * (1.0 + g * (1.0 - s)))).astype(BF16)
        gn = (up * (g * s)).astype(BF16).astype(F32)
        mean = jnp.mean(gn, axis=0, keepdims=True)
        slope = jnp.mean(gn * full, axis=0, keepdims=True)
        gret[:, at] = (inv[:, at] * (gn - mean - full * slope)).astype(BF16)
    sent = [move.start(ggate, ggate_out), move.start(gret, gret_out)]
    wait(late)

    def gate_step(at):
        gg[:, at] = dot(ggate[...], x[:, at], ((1,), (0,))).astype(BF16)

    def out_step(at):
        go[:, at] = dot(hidden[...], mid[:, at], ((1,), (0,))).astype(BF16)

    spans(x.shape[1], WIDE, gate_step)
    sent += move.kind(gg, grads_out, ("to", 0, 2), depth)
    spans(x.shape[1], WIDE, out_step)
    sent += move.kind(go, grads_out, ("to", 1, 2), depth)
    wait(sent)


def retention_backward(
    depth, q, k, v, weights, gret, x, pc, pr, sc, sr, grow, fall, packed, grads, scores
):
    seq = x.shape[0]
    part = q.shape[0] // depth
    width = v.shape[0] // depth
    pairs = 2 * part * depth

    def place(value, at, offset):
        for i in range(depth):
            z = 2 * i * part + offset
            packed[z : z + part, at] = value[i * part : (i + 1) * part]

    def query_step(at):
        raw = dot(gret[:, at], v[...], ((0,), (0,)))
        low = decayed(raw, (pc, pr), (sc, sr), grow, fall, at)
        scores[at, :] = low
        place(dot(k[...], low, ((1,), (1,))).astype(BF16), at, 0)

    def key_step(at):
        place(dot(q[...], scores[:, at], ((1,), (0,))).astype(BF16), at, part)
        packed[pairs:, at] = dot(gret[...], weights[:, at], ((1,), (0,))).astype(BF16)

    spans(seq, TILE, query_step)
    spans(seq, TILE, key_step)
    if len(grads.shape) == 2:

        def grad_step(at):
            full = dot(packed[...], x[:, at], ((1,), (0,))).astype(BF16)
            for i in range(depth):
                z = i * (2 * part + width)
                grads[z : z + 2 * part, at] = full[2 * i * part : 2 * (i + 1) * part]
                grads[z + 2 * part : z + 2 * part + width, at] = full[
                    pairs + i * width : pairs + (i + 1) * width
                ]

        spans(x.shape[1], WIDE, grad_step)
        return

    def home_step(row, carry):
        columns = grads.shape[3]
        at = pl.ds(pl.multiple_of(row * columns, columns), columns)
        full = dot(packed[...], x[:, at], ((1,), (0,))).astype(BF16)
        for i in range(depth):
            there = (i // 2, 2 * row + i % 2)
            grads[(*there, slice(0, 2 * part))] = full[2 * i * part : 2 * (i + 1) * part]
            grads[(*there, slice(2 * part, 2 * part + width))] = full[
                pairs + i * width : pairs + (i + 1) * width
            ]
        return carry

    lax.fori_loop(0, 4, home_step, 0)


def input_backward(depth, packed, w, ggate, vgo, out, wv, wg):
    unpack(vgo, (wv, wg, None), depth)
    pairs = w.shape[0]

    def step(at):
        total = dot(packed[:pairs, at], w[...], ((0,), (0,)))
        total = total + dot(packed[pairs:, at], wv[...], ((0,), (0,)))
        out[at, :] = (total + dot(ggate[:, at], wg[...], ((0,), (0,)))).astype(BF16)

    spans(packed.shape[1], TILE, step)


def body(
    block_in,
    cotangent,
    segments,
    w_query,
    w_key,
    w_value,
    w_gate,
    w_out,
    w_up,
    w_down,
    retention_norm_gain,
    retention_norm_bias,
    feedforward_norm_gain,
    feedforward_norm_bias,
):
    depth = lax.axis_size("z")
    part = block_in.shape[1]
    width = 4 * part
    own = lax.axis_index(GROUP)
    plane = lax.axis_index("z")
    tokens = block_in.shape[0] // 4
    seq = 8 * tokens

    kq = w_query.shape[1] // HEADS
    kv = w_value.shape[1] // HEADS
    order_q = head_order(w_query.shape[1])
    order_v = head_order(w_value.shape[1])

    def by_head(weight, order):
        return dot(order, weight, ((0,), (1,))).astype(BF16).reshape(HEADS, -1, part)

    def to_heads(send):
        got = lax.all_to_all(send, GROUP, split_axis=0, concat_axis=0, tiled=True)
        got = got.reshape(4, 2, send.shape[1], part).transpose(1, 2, 0, 3)
        return got.reshape(2, send.shape[1], width)

    split = 2 if kq % 16 == 0 else 1
    blocks = depth * split

    def regroup(rows, *counts):
        if split == 2:
            return rows.reshape(-1, width)
        cuts = np.cumsum((0,) + counts)
        return jnp.concatenate(
            [rows[:, cuts[i] : cuts[i + 1]].reshape(-1, width) for i in range(len(counts))]
        )

    def ungroup(rows, *counts):
        if split == 2:
            return rows.reshape(2, -1, width)
        cuts = 2 * np.cumsum((0,) + counts)
        return jnp.concatenate(
            [rows[cuts[i] : cuts[i + 1]].reshape(2, -1, width) for i in range(len(counts))], axis=1
        )

    def planes(mine):
        return lax.all_gather(mine, "z", axis=0, tiled=True)

    send_qk = jnp.concatenate([by_head(w_query, order_q), by_head(w_key, order_q)], axis=1)
    from_planes = planes(send_qk.reshape(-1, part)).reshape(depth, HEADS, -1, part)
    send_vgo = jnp.concatenate(
        [
            by_head(w_value, order_v),
            by_head(w_gate, order_v),
            dot(order_v, w_out, ((0,), (0,))).astype(BF16).reshape(HEADS, -1, part),
        ],
        axis=1,
    )
    got_vgo = to_heads(after(send_vgo, send_qk))
    mine_vgo = regroup(got_vgo, kv, kv, kv)
    all_vgo = planes(mine_vgo)

    small = jnp.concatenate(
        [
            retention_norm_gain,
            retention_norm_bias,
            feedforward_norm_gain,
            feedforward_norm_bias,
            segments.astype(F32),
        ]
    )
    small = row_gather(after(small, send_qk))
    params = small[:, : 4 * part].reshape(4, 4, part).transpose(1, 0, 2).reshape(4, width)
    segs = small[:, 4 * part :].astype(jnp.int32).reshape(depth, 8, tokens)
    block_in, cotangent = after(block_in, got_vgo), after(cotangent, got_vgo)
    stream_low, cot_own = to_wide(block_in, cotangent)
    mine_up, mine_down = to_wide(after(w_up, stream_low).T, after(w_down, stream_low))
    all_ud = planes(after(jnp.concatenate([mine_up, mine_down], axis=0), mine_vgo))
    stream = stream_low.astype(F32)
    hat_one, inv_one, norm_one = layernorm(stream, params[0], params[1])
    x_one = jnp.concatenate(group_gather(norm_one), axis=0)

    ids = lax.iota(jnp.int32, 8) ^ own
    ids = (ids % 2) * 4 + ids // 2
    picked = (ids[:, None] == lax.iota(jnp.int32, 8)[None, :])[:, :, None]
    here = (lax.iota(jnp.int32, depth) == plane)[:, None, None]
    seg_plane = jnp.sum(jnp.where(here, segs, 0), axis=0)
    seg = jnp.sum(jnp.where(picked, seg_plane[None], 0), axis=1).reshape(seq)
    pos = (ids[:, None] * tokens + lax.iota(jnp.int32, tokens)[None, :]).reshape(seq)

    loggam = jnp.log1p(-jnp.exp2(-5.0 - own.astype(F32)))
    lag = (pos - seq // 2).astype(F32) * loggam
    grow = jnp.exp(lag) * np.float32((kq * 2 * depth) ** (-0.5))
    where = (pos[:, None], pos[None, :], seg[:, None], seg[None, :])
    where = where + (grow[:, None], jnp.exp(-lag)[None, :])

    got_qk = lax.all_to_all(
        from_planes.transpose(1, 0, 2, 3), GROUP, split_axis=0, concat_axis=0, tiled=True
    ).reshape(4, 2, depth, 2, kq, part)
    order = (2, 1, 3, 4, 0, 5) if split == 2 else (2, 3, 1, 4, 0, 5)
    all_qk = got_qk.transpose(order).reshape(-1, width)
    x_one = after(x_one, mine_up, mine_down)
    keys_all, values_all = kq * 2 * depth, kv * 2 * depth
    square = 2 * seq * seq
    qkv_shape = (2 * keys_all + values_all, width)
    query, keys, weights = kernel_call(
        functools.partial(retention_scores, blocks),
        [((keys_all, seq), BF16), ((keys_all, seq), BF16), ((seq, seq), BF16)],
        [],
        2 * seq * width * all_qk.shape[0] + square * keys_all,
        all_qk,
        x_one,
        *where,
    )
    cot = group_gather(after(cot_own, x_one))
    wide = 2 * seq * width * values_all
    narrow, broad = ((values_all, seq), BF16), ((values_all, width), BF16)
    plain = ((values_all, seq), F32)
    gate, hidden, attn, values, normed, inv_group = kernel_call(
        functools.partial(gated_forward, blocks),
        [plain, narrow, ((seq, width), BF16), narrow, plain, ((1, seq), F32)],
        [broad, broad, broad],
        3 * wide + square * values_all,
        all_vgo,
        x_one,
        after(weights, cot),
    )
    middle = stream + group_reduce(attn)

    hat_two, inv_two, norm_two = layernorm(middle, params[2], params[3])
    x_two = group_gather(norm_two)
    token = swap(after(norm_two[:8, :128], all_ud), 2)
    hidden_all = all_ud.shape[0] // 2
    wide_ff = 2 * seq * width * hidden_all
    narrow, broad = ((hidden_all, seq), BF16), ((hidden_all, width), BF16)
    tall = ((seq, width), BF16)
    act, two_part, full_ud = kernel_call(
        functools.partial(feedforward, depth),
        [narrow, tall, (all_ud.shape, BF16)],
        [broad, broad, tall, tall, narrow, narrow, ((seq, hidden_all), BF16), tall, broad, broad],
        5 * wide_ff,
        all_ud,
        *x_two,
        after(cot[0], token),
        *cot[1:],
        copies=4 * depth + 17 + width // WIDE,
    )
    grad_two = group_reduce(two_part)

    def home(full):
        return lax.psum_scatter(full, "z", scatter_dimension=0, tiled=True)

    def from_units(mine):
        send = mine.reshape(-1, 4, part).transpose(1, 0, 2)
        return row_exchange(send).reshape(-1, part)

    home_ud = home(full_ud)

    back_two, grad_ffn_gain, grad_ffn_bias = layernorm_back(grad_two, hat_two, inv_two, params[2])
    grad_mid = cot_own.astype(F32) + back_two
    x_mid = group_gather(grad_mid.astype(BF16))

    narrow, broad = ((values_all, seq), BF16), ((values_all, width), BF16)
    plain = ((values_all, seq), F32)
    grad_gate, grad_ret, full_go = kernel_call(
        functools.partial(gated_backward, blocks),
        [narrow, narrow, ((2 * values_all, width), BF16)],
        [broad, tall, tall, plain, plain, ((1, seq), F32), narrow, narrow, narrow, broad, broad],
        3 * wide,
        all_vgo,
        x_one,
        *x_mid,
        gate,
        normed,
        inv_group,
        hidden,
        copies=3 * blocks + 15,
    )
    home_go = home(full_go)
    home_shape = (depth, 8, 2 * kq + kv, part) if split == 2 else qkv_shape
    grad_qkv, full_qkv = kernel_call(
        functools.partial(retention_backward, blocks),
        [((qkv_shape[0], seq), BF16), (home_shape, BF16)],
        [((seq, seq), BF16)],
        2 * seq * width * qkv_shape[0] + 2 * square * (keys_all + values_all),
        query,
        keys,
        values,
        weights,
        grad_ret,
        x_one,
        *where,
    )
    home_qkv = home(full_qkv)
    half = home_ud.shape[0] // 2
    grad_up, grad_down = from_wide(home_ud[:half], home_ud[half:])
    (one_part,) = kernel_call(
        functools.partial(input_backward, blocks),
        [((seq, width), BF16)],
        [broad, broad],
        2 * seq * width * qkv_shape[0] + wide,
        grad_qkv,
        all_qk,
        after(grad_gate, full_qkv, grad_up),
        all_vgo,
    )
    grad_one = group_reduce(one_part)
    (ffn_part,) = kernel_call(
        functools.partial(down_forward, depth),
        [((seq, width), BF16)],
        [((hidden_all, width), BF16)],
        wide_ff,
        all_ud,
        after(act, one_part),
    )
    ffn = group_reduce(ffn_part)
    back_one, grad_attn_gain, grad_attn_bias = layernorm_back(grad_one, hat_one, inv_one, params[0])
    totals = total_over_all(
        jnp.stack([grad_attn_gain, grad_attn_bias, grad_ffn_gain, grad_ffn_bias])
    )
    totals = lax.dynamic_slice_in_dim(totals, lax.axis_index(ROW) * part, part, 1)
    grad_in, block_out = from_wide(
        (grad_mid + back_one).astype(BF16), (middle + ffn).astype(BF16)
    )
    grad_in = grad_in.astype(F32)

    def from_heads(mine):
        send = mine.reshape(2, -1, 4, part).transpose(2, 0, 1, 3).reshape(8, -1, part)
        return lax.all_to_all(send, GROUP, split_axis=0, concat_axis=0, tiled=True)

    def columns(grads, order):
        return dot(grads.reshape(-1, part), order, ((0,), (1,)))

    go = from_heads(ungroup(after(home_go, grad_in), kv, kv))
    home_qkv = after(home_qkv, go, totals)
    if split == 2:
        home_qkv = home_qkv.reshape(8, 2 * kq + kv, part)
        back = lax.all_to_all(home_qkv, GROUP, split_axis=0, concat_axis=0, tiled=True)
    else:
        back = from_heads(ungroup(home_qkv, kq, kq, kv))
    grad_up, grad_down = grad_up.T.astype(F32), grad_down.astype(F32)
    out_gate = columns(go[:, :kv], order_v)
    out_out = dot(order_v, go[:, kv:].reshape(-1, part), ((1,), (0,)))
    out_query = columns(back[:, :kq], order_q)
    out_key = columns(back[:, kq : 2 * kq], order_q)
    out_value = columns(back[:, 2 * kq :], order_v)
    return (
        block_out,
        grad_in,
        out_query,
        out_key,
        out_value,
        out_gate,
        out_out,
        grad_up,
        grad_down,
        totals[0],
        totals[1],
        totals[2],
        totals[3],
    )


def solution(mesh):
    rows, cols = mesh.devices.shape
    fine = Mesh(mesh.devices.reshape(rows // 2, 2, cols // 2, 2), ("x", "k", "z", "y"))
    row, col = ("x", "k"), ("z", "y")
    tok, unit = P(col, row), P(row, col)
    return jax.shard_map(
        body,
        mesh=fine,
        in_specs=(tok, tok, P(row), unit, unit, unit, unit, tok, unit, tok)
        + (P(row),) * 4,
        out_specs=(tok, tok, unit, unit, unit, unit, tok, unit, tok) + (P(row),) * 4,
        check_vma=False,
    )
```
